128 devices in a mesh: dp: 4 (over z), tensor: 32 (over y, x, core).
Axes of the slice: x: 4, y: 4, z: 4, core: 2. Of those that a mesh axis runs over, the one named last changes fastest.
Arguments:
- activations: bfloat16 [8192, 8192], P('dp', 'tensor'), may hold values from -6 to 6
- out_grads: bfloat16 [8192, 28672], P('dp', 'tensor'), may hold values from -6 to 6
- query_inputs: bfloat16 [8192, 2048], P('tensor', 'dp'), may hold values from -0.125 to 0.125
- query_outputs: bfloat16 [28672, 2048], P('tensor', 'dp'), may hold values from -0.0625 to 0.0625
Outputs:
- scores: float32 [8192, 64], P('dp', 'tensor')
The draws below stay inside these ranges and needn't reach their ends.
All inputs are finite; a program needn't handle non-finite values.
Results may differ from the reference program's by a relative error of at most 0.0003.
Values may be sent and summed in bfloat16 or wider, within the bound.
A program may use at most 192 MiB of HBM per device.

```python
import math
import jax
import jax.numpy as jnp
from jax import lax

DIN = 8192
DOUT = 28672
NQ = 64
R = 32
TOKENS = 8192


def raised(values, key, source, target, parts, factor):
    owner, partner = [(jnp.arange(values.shape[dim]) // (values.shape[dim] // parts)).reshape([-1 if axis == dim else 1 for axis in range(values.ndim)]) for dim in (source, target)]
    chosen = jax.random.permutation(key, parts)[partner]
    strong = (owner == chosen) | (owner == (partner + parts // 2) % parts)
    return jnp.where(strong, factor * values, values)


def level_of(stream_key, extent, pieces, low, top_value):
    factor_of, own = 1.0, jax.random.fold_in(stream_key, 6)
    for dim, shards_of in pieces:
        heights = jnp.exp(jax.random.uniform(jax.random.fold_in(own, dim), (shards_of,), jnp.float32, low / len(pieces), top_value / len(pieces)))
        factor_of = factor_of * jnp.repeat(heights, extent[dim] // shards_of).reshape([-1 if axis == dim else 1 for axis in range(len(extent))])
    return factor_of


def noise(rng, dims, deviation, bound, pieces=(), held_as=jnp.bfloat16):
    array = deviation * jax.random.normal(rng, dims, jnp.float32)
    if pieces:
        array = array * level_of(rng, dims, pieces, -0.22, 0.18)
    return jnp.clip(array, -bound, bound).astype(held_as)


def bell_draw_with(stream_key, shape, width, limit, pieces, heavy, held_as=jnp.bfloat16):
    values = width * jax.random.normal(stream_key, shape, jnp.float32)
    if pieces:
        values = values * level_of(stream_key, shape, pieces, -0.22, 0.18)
    return jnp.clip(raised(values, jax.random.fold_in(stream_key, 3), *heavy), -limit, limit).astype(held_as)


def setup_inputs(seed: int = 0) -> dict:
    streams_of = jax.random.split(jax.random.key(seed), 5)
    return {
        "activations": noise(streams_of[0], (TOKENS, DIN), 1.0, 6.0, ((0, 4), (1, 32))),
        "out_grads": noise(streams_of[1], (TOKENS, DOUT), 1.0, 6.0, ((0, 4), (1, 32))),
        "query_inputs": bell_draw_with(streams_of[2], (DIN, NQ * R), DIN ** -0.5, 0.125, ((0, 32), (1, 4)), (0, 1, 32, 2.75)),
        "query_outputs": bell_draw_with(streams_of[3], (DOUT, NQ * R), DOUT ** -0.5, 0.0625, ((0, 32), (1, 4)), (0, 1, 32, 2.75)),
    }


def reference(activations, out_grads, query_inputs, query_outputs):
    block = math.gcd(TOKENS, 1024)
    act_blocks = activations.reshape(TOKENS // block, block, DIN)
    grad_blocks = out_grads.reshape(TOKENS // block, block, DOUT)

    def one_block(pair):
        left = jnp.dot(pair[0], query_inputs, preferred_element_type=jnp.float32)
        right = jnp.dot(pair[1], query_outputs, preferred_element_type=jnp.float32)
        return (left * right).reshape(block, NQ, R).sum(axis=-1) * (1.0 / math.sqrt(R))
    scores = lax.map(one_block, (act_blocks, grad_blocks))
    return scores.reshape(TOKENS, NQ)
```

```python
import functools
import math

import jax
import jax.numpy as jnp
from jax import lax
from jax.experimental import pallas as pl
from jax.experimental.pallas import tpu as pltpu
from jax.sharding import PartitionSpec as P

R = 32
MESH = pl.DeviceIdType.MESH
BF16, F32 = jnp.bfloat16, jnp.float32
SPAN, LOW = 250.0, -124.0
ORDER = (2, 1, 3, 0)
STEP_X, STEP_Y, LAST_Y, LAST_X = 0, 24, 48, 54


def encode(value, box):
    rows = value.shape[0]
    size = jnp.abs(value).reshape(rows // 8, 8, 128)
    top = jnp.max(size, axis=0)
    top = jnp.concatenate([top, top], axis=0).astype(BF16)
    inverse = 1.0 / jnp.maximum(top.astype(F32)[:8], 1e-30)
    part = size * inverse[None]
    root = part * lax.rsqrt(part + 1e-30)
    code = jnp.exp2(root * SPAN + LOW).reshape(rows, 128)
    box[pl.ds(0, rows), :] = jnp.where(value < 0, -code, code).astype(BF16)
    box[pl.ds(rows, 16), :] = top


def decode(box):
    rows = box.shape[0] - 16
    code = box[pl.ds(0, rows), :].astype(F32)
    top = box[pl.ds(rows, 16), :].astype(F32)[:8]
    root = jnp.log(jnp.abs(code)) * (1.0 / (SPAN * math.log(2.0))) - LOW / SPAN
    size = ((root * root).reshape(rows // 8, 8, 128) * top[None]).reshape(rows, 128)
    return jnp.where(code < 0, -size, size)


def kernel(
    act, grad, q_in, q_out, out,
    a, q, part, last, sent, got, mine, theirs,
    load_sem, a_send, a_recv, z_send, z_recv, core_send, core_recv, send_sem, recv_sem, end_send, end_recv,
):
    z, t = lax.axis_index("dp"), lax.axis_index("tensor")
    core, x, y = t % 2, (t // 2) % 4, t // 8
    tokens, w_in = act.shape
    w_out = grad.shape[1]
    half, wide = tokens // 2, w_in + w_out
    rows = half // 4

    def at(dx=0, dy=0, dz=0, other=False):
        index = (((y + dy + 4) % 4) * 4 + (x + dx + 4) % 4) * 2 + ((1 - core) if other else core)
        return ((z + dz + 4) % 4, index)

    own, partner_rows = core * half, (1 - core) * half

    loads = [
        pltpu.make_async_copy(act.at[pl.ds(own, half), :], a.at[:, pl.ds(0, w_in)], load_sem.at[0]),
        pltpu.make_async_copy(grad.at[pl.ds(own, half), :], a.at[:, pl.ds(w_in, w_out)], load_sem.at[1]),
    ]
    for j, step in enumerate(ORDER):
        columns = pl.ds(pl.multiple_of(((x + step) % 4) * 128, 128), 128)
        loads.append(pltpu.make_async_copy(q_in.at[:, columns], q.at[j, z, pl.ds(0, w_in), :], load_sem.at[2 + 2 * j]))
        loads.append(pltpu.make_async_copy(q_out.at[:, columns], q.at[j, z, pl.ds(w_in, w_out), :], load_sem.at[3 + 2 * j]))
    for load in loads:
        load.start()

    barrier = pltpu.get_barrier_semaphore()
    for device in (at(dx=1), at(dx=-1), at(dy=1), at(dy=-1), at(dz=1), at(dz=-1), at(other=True)):
        pl.semaphore_signal(barrier, inc=1, device_id=device, device_id_type=MESH)
    pl.semaphore_wait(barrier, 7)

    def copy(src, dst, send, recv, device):
        return pltpu.make_async_remote_copy(
            src_ref=src, dst_ref=dst, send_sem=send, recv_sem=recv, device_id=device, device_id_type=MESH)

    swaps = [
        copy(act.at[pl.ds(partner_rows, half), :], a.at[:, pl.ds(wide, w_in)], a_send.at[0], a_recv.at[0], at(other=True)),
        copy(grad.at[pl.ds(partner_rows, half), :], a.at[:, pl.ds(wide + w_in, w_out)], a_send.at[1], a_recv.at[1], at(other=True)),
    ]

    def z_copy(j, kind):
        piece, low, count, dz = {
            0: (z, 0, wide, 1),
            1: (z, 0, wide, -1),
            2: ((z + 3) % 4, 0, wide // 2, 1),
            3: ((z + 1) % 4, wide // 2, wide // 2, -1),
        }[kind]
        ref = q.at[j, piece, pl.ds(low, count), :]
        return copy(ref, ref, z_send.at[j, kind], z_recv.at[j, kind], at(dz=dz))

    def z_arrival(j, kind):
        piece, low, count, dz = {
            0: ((z + 3) % 4, 0, wide, 1),
            1: ((z + 1) % 4, 0, wide, -1),
            2: ((z + 2) % 4, 0, wide // 2, 1),
            3: ((z + 2) % 4, wide // 2, wide // 2, -1),
        }[kind]
        ref = q.at[j, piece, pl.ds(low, count), :]
        return copy(ref, ref, z_send.at[j, kind], z_recv.at[j, kind], at(dz=dz))

    def core_copy(j, step):
        piece = (z + step) % 4
        return copy(q.at[j, piece, pl.ds(0, wide), :], q.at[j, piece, pl.ds(wide, wide), :],
                    core_send.at[j, step], core_recv.at[j, step], at(other=True))

    for swap in swaps:
        swap.start()
    for j in range(4):
        loads[2 + 2 * j].wait()
        loads[3 + 2 * j].wait()
        z_copy(j, 0).start()
        z_copy(j, 1).start()
        core_copy(j, 0).start()
    loads[0].wait()
    loads[1].wait()

    def pass_near(j):
        z_arrival(j, 0).wait_recv()
        z_copy(j, 2).start()
        core_copy(j, 3).start()
        z_arrival(j, 1).wait_recv()
        z_copy(j, 3).start()
        core_copy(j, 1).start()

    def pass_far(j):
        z_arrival(j, 2).wait_recv()
        z_arrival(j, 3).wait_recv()
        core_copy(j, 2).start()

    def await_core(j):
        for step in (0, 3, 1, 2):
            core_copy(j, step).wait_recv()

    def project(j):
        @pl.loop(0, 4)
        def _(i):
            pair, twin = i // 2, i % 2
            line = pl.ds(pl.multiple_of(pair * 2 * rows, 2 * rows), 2 * rows)

            def product(low, count):
                total = None
                for base in (low, low + wide):
                    left = a[line, pl.ds(base, count)]
                    right = jnp.concatenate([q[j, 2 * twin, pl.ds(base, count), :], q[j, 2 * twin + 1, pl.ds(base, count), :]], axis=1)
                    term = jnp.dot(left, right, preferred_element_type=F32)
                    total = term if total is None else total + term
                return total

            for h, (low, count) in enumerate(((0, w_in), (w_in, w_out))):
                value = product(low, count)
                for g in range(2):
                    for n in range(2):
                        part[j, 2 * pair + g, 2 * twin + n, h] = value[g * rows:(g + 1) * rows, n * 128:(n + 1) * 128]

    def message(m, device):
        return copy(sent.at[m], got.at[m], send_sem.at[m], recv_sem.at[m], device)

    def arrived(m):
        message(m, at(dx=1)).wait_recv()

    def send(m, source, device, add=None):
        if add is not None:
            arrived(add)

        @pl.loop(0, 2)
        def _(h):
            value = source[h]
            if add is not None:
                value = value + decode(got.at[add, h])
            encode(value, sent.at[m, h])

        message(m, device).start()

    def finish(target, source, first, second):
        arrived(first)
        arrived(second)

        @pl.loop(0, 2)
        def _(h):
            target[h] = source[h] + decode(got.at[first, h]) + decode(got.at[second, h])

    def along_y(base, stride, j, source, target):
        up, down = at(dy=1), at(dy=-1)
        far, after, before = (y + 2) % 4, (y + 1) % 4, (y + 3) % 4
        slot = lambda kind: base + kind * stride + j
        send(slot(0), source(0, far), up)
        send(slot(3), source(1, far), down)
        send(slot(2), source(1, after), up)
        send(slot(5), source(0, before), down)
        send(slot(1), source(0, after), up, add=slot(0))
        send(slot(4), source(1, before), down, add=slot(3))
        finish(target(0), source(0, y), slot(1), slot(5))
        finish(target(1), source(1, y), slot(4), slot(2))

    def step_x(kind, g, n, j, add=None):
        device = at(dx=1) if kind < 3 else at(dx=-1)
        send(STEP_X + kind * 4 + n, part.at[j, g, n], device, add=None if add is None else STEP_X + add * 4 + n)

    for swap in swaps:
        swap.wait_recv()
    right, left = at(dx=1), at(dx=-1)
    for j in range(4):
        pass_near(j)
        pass_far(j)
        await_core(j)
        project(j)

        @pl.loop(0, 4)
        def _(n):
            if ORDER[j] == 2:
                step_x(0, 0, n, j)
                step_x(3, 1, n, j)
            elif ORDER[j] == 1:
                step_x(2, 1, n, j)
                step_x(1, 0, n, j, add=0)
            elif ORDER[j] == 3:
                step_x(5, 0, n, j)
                step_x(4, 1, n, j, add=3)
            else:
                finish(part.at[j, 0, n], part.at[j, 0, n], STEP_X + 1 * 4 + n, STEP_X + 5 * 4 + n)
                finish(part.at[j, 1, n], part.at[j, 1, n], STEP_X + 4 * 4 + n, STEP_X + 2 * 4 + n)

        along_y(STEP_Y, 4, j, lambda b, n: part.at[j, 2 + b, n], lambda b: last.at[j, b])
        if ORDER[j] == 2:
            send(LAST_X + 0, last.at[j, 0], right)
            send(LAST_X + 3, last.at[j, 1], left)
        elif ORDER[j] == 1:
            send(LAST_X + 2, last.at[j, 1], right)
            send(LAST_X + 1, last.at[j, 0], right, add=LAST_X + 0)
        elif ORDER[j] == 3:
            send(LAST_X + 5, last.at[j, 0], left)
            send(LAST_X + 4, last.at[j, 1], left, add=LAST_X + 3)
        else:
            finish(last.at[j, 0], last.at[j, 0], LAST_X + 1, LAST_X + 5)
            finish(last.at[j, 1], last.at[j, 1], LAST_X + 4, LAST_X + 2)
            along_y(LAST_Y, 1, 0, lambda b, n: part.at[j, b, n], lambda b: last.at[0, b])

    query = lax.broadcasted_iota(jnp.int32, (8, 128), 0)
    owner = lax.broadcasted_iota(jnp.int32, (8, 128), 1) // R

    def pick(which):
        return jnp.where((owner == query + 2 * which) & (query < 2), 1.0, 0.0).astype(BF16)

    for g in range(4):
        value = last.at[0 if g < 2 else 3, g % 2]
        product = value[0] * value[1] * (1.0 / math.sqrt(R))
        high = product.astype(BF16)
        rest = product - high.astype(F32)
        middle = rest.astype(BF16)
        low = (rest - middle.astype(F32)).astype(BF16)
        for which, target in ((core, mine), (1 - core, theirs)):
            mask = pick(which)
            total = None
            for term in (low, middle, high):
                s = lax.dot_general(mask, term, (((1,), (1,)), ((), ())), preferred_element_type=F32)
                total = s if total is None else total + s
            target[0, :, pl.ds(g * rows, rows)] = total
    final = copy(theirs.at[0], theirs.at[1], end_send, end_recv, at(other=True))
    final.start()
    out[:, pl.ds(pl.multiple_of(own, half), half)] = mine[0]
    final.wait_recv()
    out[:, pl.ds(pl.multiple_of(partner_rows, half), half)] = theirs[1]

    final.wait_send()
    for swap in swaps:
        swap.wait_send()
    for j in range(4):
        for k in range(4):
            z_copy(j, k).wait_send()
            core_copy(j, k).wait_send()

    @pl.loop(0, 60)
    def _(m):
        message(m, right).wait_send()


def scores_of(act, grad, q_in, q_out):
    tokens, w_in = act.shape
    w_out = grad.shape[1]
    half, wide = tokens // 2, w_in + w_out
    rows = half // 4
    dma = pltpu.SemaphoreType.DMA
    scores = pl.pallas_call(
        kernel,
        out_shape=jax.ShapeDtypeStruct((8, tokens), F32),
        in_specs=[pl.BlockSpec(memory_space=pl.ANY)] * 4,
        out_specs=pl.BlockSpec(memory_space=pltpu.VMEM),
        scratch_shapes=[
            pltpu.VMEM((half, 2 * wide), BF16),
            pltpu.VMEM((4, 4, 2 * wide, 128), BF16),
            pltpu.VMEM((4, 4, 4, 2, rows, 128), F32),
            pltpu.VMEM((4, 2, 2, rows, 128), F32),
            pltpu.VMEM((60, 2, rows + 16, 128), BF16),
            pltpu.VMEM((60, 2, rows + 16, 128), BF16),
            pltpu.VMEM((1, 8, half), F32),
            pltpu.VMEM((2, 8, half), F32),
            dma((10,)), dma((2,)), dma((2,)),
            dma((4, 4)), dma((4, 4)), dma((4, 4)), dma((4, 4)),
            dma((60,)), dma((60,)), dma, dma,
        ],
        compiler_params=pltpu.CompilerParams(
            collective_id=0, has_side_effects=True, vmem_limit_bytes=58 * 1024 * 1024),
        cost_estimate=pl.CostEstimate(flops=2 * tokens * wide * 2048, bytes_accessed=6 * 2**20, transcendentals=0),
    )(act, grad, q_in, q_out)
    return scores[:2].T


def solution(mesh):
    return jax.shard_map(
        scores_of,
        mesh=mesh,
        in_specs=(P("dp", "tensor"), P("dp", "tensor"), P("tensor", "dp"), P("tensor", "dp")),
        out_specs=P("dp", "tensor"),
        check_vma=False,
    )
```

```python
import functools
import math

import jax
import jax.numpy as jnp
from jax import lax
from jax.experimental import pallas as pl
from jax.experimental.pallas import tpu as pltpu
from jax.sharding import PartitionSpec as P

R = 32
MESH = pl.DeviceIdType.MESH
BF16, F32 = jnp.bfloat16, jnp.float32
SPAN, LOW = 250.0, -124.0
ORDER = (2, 1, 3, 0)
ROWS_X = 288
TASKS = (
    ('own', 0), ('own', 1), ('near', 0), ('xr', 2, 0), ('xr', 1, 0), ('xr', 3, 0), ('pn', 0), ('xr', 2, 1),
    ('xr', 2, 3), ('near', 1), ('xa', 1, 0), ('xa', 3, 0), ('pn', 1), ('far', 0), ('xr', 1, 1), ('xr', 1, 3),
    ('pf', 0), ('xr', 2, 2), ('xa', 1, 1), ('yr', 0), ('near', 2), ('xa', 1, 3), ('pn', 2), ('far', 1), ('xr', 3, 3),
    ('xr', 3, 1), ('ya', 1, 0), ('ya', 3, 0), ('xa', 3, 3), ('pf', 1), ('yr', 1), ('xr', 1, 2), ('xa', 3, 1),
    ('xf', 0), ('near', 3), ('yf', 0), ('lx', 0), ('pn', 3), ('far', 2), ('ya', 1, 1), ('ya', 3, 1), ('xa', 1, 2),
    ('pf', 2), ('yr', 2), ('xr', 3, 2), ('xa', 3, 2), ('far', 3), ('yf', 1), ('lx', 2), ('pf', 3), ('yr', 3),
    ('ya', 3, 2), ('xf', 3), ('xf', 1), ('ya', 1, 2), ('lx', 1), ('ya', 1, 3), ('ya', 3, 3), ('xf', 2), ('ly', 0),
    ('yf', 2), ('lx', 4), ('lx', 5), ('yf', 3), ('ly', 1), ('ly', 4), ('lx', 9), ('ly', 9),
)


def encode(value, box):
    rows = value.shape[0]
    size = jnp.abs(value).reshape(rows // 8, 8, 128)
    top = jnp.max(size, axis=0)
    top = jnp.concatenate([top, top], axis=0).astype(BF16)
    inverse = 1.0 / jnp.maximum(top.astype(F32)[:8], 1e-30)
    part = size * inverse[None]
    root = part * lax.rsqrt(part + 1e-30)
    code = jnp.exp2(root * SPAN + LOW).reshape(rows, 128)
    box[pl.ds(0, rows), :] = jnp.where(value < 0, -code, code).astype(BF16)
    box[pl.ds(rows, 16), :] = top


def decode(box):
    rows = box.shape[0] - 16
    code = box[pl.ds(0, rows), :].astype(F32)
    top = box[pl.ds(rows, 16), :].astype(F32)[:8]
    root = jnp.log(jnp.abs(code)) * (1.0 / (SPAN * math.log(2.0))) - LOW / SPAN
    size = ((root * root).reshape(rows // 8, 8, 128) * top[None]).reshape(rows, 128)
    return jnp.where(code < 0, -size, size)


def kernel(
    act, grad, q_in, q_out, out,
    a, q, part, sent_x, got_x, sent_y, got_y, mine, theirs,
    load_sem, a_send, a_recv, z_send, z_recv, core_send, core_recv,
    send_x_sem, recv_x_sem, send_y_sem, recv_y_sem, end_send, end_recv,
):
    box_x, box_y = (sent_x, got_x, send_x_sem, recv_x_sem), (sent_y, got_y, send_y_sem, recv_y_sem)
    z, t = lax.axis_index("dp"), lax.axis_index("tensor")
    core, x, y = t % 2, (t // 2) % 4, t // 8
    tokens, w_in = act.shape
    w_out = grad.shape[1]
    half, wide = tokens // 2, w_in + w_out
    rx, ry = ROWS_X, half // 2 - ROWS_X

    def at(dx=0, dy=0, dz=0, other=False):
        index = (((y + dy + 4) % 4) * 4 + (x + dx + 4) % 4) * 2 + ((1 - core) if other else core)
        return ((z + dz + 4) % 4, index)

    own, partner_rows = core * half, (1 - core) * half

    loads = [
        pltpu.make_async_copy(act.at[pl.ds(own, half), :], a.at[:, pl.ds(0, w_in)], load_sem.at[0]),
        pltpu.make_async_copy(grad.at[pl.ds(own, half), :], a.at[:, pl.ds(w_in, w_out)], load_sem.at[1]),
    ]
    for j, step in enumerate(ORDER):
        columns = pl.ds(pl.multiple_of(((x + step) % 4) * 128, 128), 128)
        loads.append(pltpu.make_async_copy(q_in.at[:, columns], q.at[j, z, pl.ds(0, w_in), :], load_sem.at[2 + 2 * j]))
        loads.append(pltpu.make_async_copy(q_out.at[:, columns], q.at[j, z, pl.ds(w_in, w_out), :], load_sem.at[3 + 2 * j]))
    for load in loads:
        load.start()

    barrier = pltpu.get_barrier_semaphore()
    for device in (at(dx=1), at(dx=-1), at(dy=1), at(dy=-1), at(dz=1), at(dz=-1), at(other=True)):
        pl.semaphore_signal(barrier, inc=1, device_id=device, device_id_type=MESH)
    pl.semaphore_wait(barrier, 7)

    def copy(src, dst, send, recv, device):
        return pltpu.make_async_remote_copy(
            src_ref=src, dst_ref=dst, send_sem=send, recv_sem=recv, device_id=device, device_id_type=MESH)

    swaps = [
        copy(act.at[pl.ds(partner_rows, half), :], a.at[:, pl.ds(wide, w_in)], a_send.at[0], a_recv.at[0], at(other=True)),
        copy(grad.at[pl.ds(partner_rows, half), :], a.at[:, pl.ds(wide + w_in, w_out)], a_send.at[1], a_recv.at[1], at(other=True)),
    ]

    def z_copy(j, kind):
        piece, low, count, dz = {
            0: (z, 0, wide, 1),
            1: (z, 0, wide, -1),
            2: ((z + 3) % 4, 0, wide // 2, 1),
            3: ((z + 1) % 4, wide // 2, wide // 2, -1),
        }[kind]
        ref = q.at[j, piece, pl.ds(low, count), :]
        return copy(ref, ref, z_send.at[j, kind], z_recv.at[j, kind], at(dz=dz))

    def z_arrival(j, kind):
        piece, low, count, dz = {
            0: ((z + 3) % 4, 0, wide, 1),
            1: ((z + 1) % 4, 0, wide, -1),
            2: ((z + 2) % 4, 0, wide // 2, 1),
            3: ((z + 2) % 4, wide // 2, wide // 2, -1),
        }[kind]
        ref = q.at[j, piece, pl.ds(low, count), :]
        return copy(ref, ref, z_send.at[j, kind], z_recv.at[j, kind], at(dz=dz))

    def core_copy(j, step):
        piece = (z + step) % 4
        return copy(q.at[j, piece, pl.ds(0, wide), :], q.at[j, piece, pl.ds(wide, wide), :],
                    core_send.at[j, step], core_recv.at[j, step], at(other=True))

    for j in range(4):
        loads[2 + 2 * j].wait()
        loads[3 + 2 * j].wait()
        if j < 2:
            z_copy(j, 0).start()
            z_copy(j, 1).start()
        core_copy(j, 0).start()
        if j == 1:
            for swap in swaps:
                swap.start()

    def pass_near(j):
        z_arrival(j, 0).wait_recv()
        z_copy(j, 2).start()
        core_copy(j, 3).start()
        z_arrival(j, 1).wait_recv()
        z_copy(j, 3).start()
        core_copy(j, 1).start()
        if j < 2:
            z_copy(j + 2, 0).start()
            z_copy(j + 2, 1).start()

    def pass_far(j):
        z_arrival(j, 2).wait_recv()
        z_arrival(j, 3).wait_recv()
        core_copy(j, 2).start()

    def project(pieces):
        for j, i in pieces:
            core_copy(j, i).wait_recv()
        block = half // 2

        @pl.loop(0, 2)
        def _(i):
            line = pl.ds(pl.multiple_of(i * block, block), block)
            for h, (low, count) in enumerate(((0, w_in), (w_in, w_out))):
                total = None
                for base in (low, low + wide):
                    right = [q[j, (z + step) % 4, pl.ds(base, count), :] for j, step in pieces]
                    right = right[0] if len(right) == 1 else jnp.concatenate(right, axis=1)
                    term = jnp.dot(a[line, pl.ds(base, count)], right, preferred_element_type=F32)
                    total = term if total is None else total + term
                for k, (j, step) in enumerate(pieces):
                    part[j, (z + step) % 4, h, line, :] = total[:, k * 128:(k + 1) * 128]

    def message(box, m, device):
        sent, got, out_sem, in_sem = box
        return copy(sent.at[m], got.at[m], out_sem.at[m], in_sem.at[m], device)

    def arrived(box, m):
        message(box, m, at(dx=1)).wait_recv()

    def send(box, m, source, device, add=None):
        sent, got = box[:2]
        if add is not None:
            arrived(box, add)

        @pl.loop(0, 2)
        def _(h):
            value = source[h]
            if add is not None:
                value = value + decode(got.at[add, h])
            encode(value, sent.at[m, h])

        message(box, m, device).start()

    def finish(box, target, first, second):
        got = box[1]
        arrived(box, first)
        arrived(box, second)

        @pl.loop(0, 2)
        def _(h):
            target[h] = target[h] + decode(got.at[first, h]) + decode(got.at[second, h])

    right, left = at(dx=1), at(dx=-1)
    up, down = at(dy=1), at(dy=-1)

    def x_part(j, n, b):
        return part.at[j, n, :, pl.ds(b * rx, rx), :]

    def y_part(j, n, b):
        return part.at[j, n, :, pl.ds(2 * rx + b * ry, ry), :]

    def send_x(kind, j, n, b, add=None):
        send(box_x, kind * 4 + n, x_part(j, n, b), right if kind < 3 else left, None if add is None else add * 4 + n)

    def send_y(kind, j, n, b, add=None):
        send(box_y, kind * 4 + j, y_part(j, n, b), up if kind < 3 else down, None if add is None else add * 4 + j)

    def last_x(kind, j, b, add=None):
        send(box_y, 24 + kind, y_part(j, y, b), right if kind < 3 else left, None if add is None else 24 + add)

    def last_y(kind, n, b, add=None):
        send(box_x, 24 + kind, x_part(3, n, b), up if kind < 3 else down, None if add is None else 24 + add)

    far, after, before = (y + 2) % 4, (y + 1) % 4, (y + 3) % 4

    def task(name, *index):
        if name == "near":
            pass_near(index[0])
        elif name == "far":
            pass_far(index[0])
        elif name == "own":
            if index[0] == 0:
                for load in loads[:2]:
                    load.wait()
                for swap in swaps:
                    swap.wait_recv()
            pieces = [(2 * index[0], 0), (2 * index[0] + 1, 0)]
            project(pieces)
        elif name == "pn":
            project([(index[0], 3), (index[0], 1)])
        elif name == "pf":
            project([(index[0], 2)])
        elif name == "xr":
            kind, i = index
            n = (z + i) % 4
            if kind == 2:
                send_x(0, 0, n, 0)
                send_x(3, 0, n, 1)
            elif kind == 1:
                send_x(2, 1, n, 1)
            else:
                send_x(5, 2, n, 0)
        elif name == "xa":
            kind, i = index
            n = (z + i) % 4
            if kind == 1:
                send_x(1, 1, n, 0, add=0)
            else:
                send_x(4, 2, n, 1, add=3)
        elif name == "xf":
            n = (z + index[0]) % 4
            finish(box_x, x_part(3, n, 0), 4 + n, 20 + n)
            finish(box_x, x_part(3, n, 1), 16 + n, 8 + n)
        elif name == "yr":
            j = index[0]
            send_y(0, j, far, 0)
            send_y(3, j, far, 1)
            send_y(2, j, after, 1)
            send_y(5, j, before, 0)
        elif name == "ya":
            kind, j = index
            if kind == 1:
                send_y(1, j, after, 0, add=0)
            else:
                send_y(4, j, before, 1, add=3)
        elif name == "yf":
            j = index[0]
            finish(box_y, y_part(j, y, 0), 4 + j, 20 + j)
            finish(box_y, y_part(j, y, 1), 16 + j, 8 + j)
        elif name == "lx":
            kind = index[0]
            if kind == 0:
                last_x(0, 0, 0)
                last_x(3, 0, 1)
            elif kind == 2:
                last_x(2, 1, 1)
            elif kind == 5:
                last_x(5, 2, 0)
            elif kind == 1:
                last_x(1, 1, 0, add=0)
            elif kind == 4:
                last_x(4, 2, 1, add=3)
            else:
                finish(box_y, y_part(3, y, 0), 24 + 1, 24 + 5)
                finish(box_y, y_part(3, y, 1), 24 + 4, 24 + 2)
        else:
            kind = index[0]
            if kind == 0:
                last_y(0, far, 0)
                last_y(3, far, 1)
                last_y(2, after, 1)
                last_y(5, before, 0)
            elif kind == 1:
                last_y(1, after, 0, add=0)
            elif kind == 4:
                last_y(4, before, 1, add=3)
            else:
                finish(box_x, x_part(3, y, 0), 24 + 1, 24 + 5)
                finish(box_x, x_part(3, y, 1), 24 + 4, 24 + 2)

    for name, *index in TASKS:
        task(name, *index)

    query = lax.broadcasted_iota(jnp.int32, (8, 128), 0)
    owner = lax.broadcasted_iota(jnp.int32, (8, 128), 1) // R

    def pick(which):
        return jnp.where((owner == query + 2 * which) & (query < 2), 1.0, 0.0).astype(BF16)

    rows = half // 4
    for g in range(4):
        line = pl.ds(g * rows, rows)
        product = part[3, y, 0, line, :] * part[3, y, 1, line, :] * (1.0 / math.sqrt(R))
        high = product.astype(BF16)
        rest = product - high.astype(F32)
        middle = rest.astype(BF16)
        low = (rest - middle.astype(F32)).astype(BF16)
        for which, target in ((core, mine), (1 - core, theirs)):
            mask = pick(which)
            total = None
            for term in (low, middle, high):
                s = lax.dot_general(mask, term, (((1,), (1,)), ((), ())), preferred_element_type=F32)
                total = s if total is None else total + s
            target[0, :, pl.ds(g * rows, rows)] = total
    final = copy(theirs.at[0], theirs.at[1], end_send, end_recv, at(other=True))
    final.start()
    out[:, pl.ds(pl.multiple_of(own, half), half)] = mine[0]
    final.wait_recv()
    out[:, pl.ds(pl.multiple_of(partner_rows, half), half)] = theirs[1]

    final.wait_send()
    for swap in swaps:
        swap.wait_send()
    for j in range(4):
        for k in range(4):
            z_copy(j, k).wait_send()
            core_copy(j, k).wait_send()

    @pl.loop(0, 30)
    def _(m):
        message(box_x, m, right).wait_send()
        message(box_y, m, right).wait_send()


def scores_of(act, grad, q_in, q_out):
    tokens, w_in = act.shape
    w_out = grad.shape[1]
    half, wide = tokens // 2, w_in + w_out
    rx, ry = ROWS_X, half // 2 - ROWS_X
    dma = pltpu.SemaphoreType.DMA
    scores = pl.pallas_call(
        kernel,
        out_shape=jax.ShapeDtypeStruct((8, tokens), F32),
        in_specs=[pl.BlockSpec(memory_space=pl.ANY)] * 4,
        out_specs=pl.BlockSpec(memory_space=pltpu.VMEM),
        scratch_shapes=[
            pltpu.VMEM((half, 2 * wide), BF16),
            pltpu.VMEM((4, 4, 2 * wide, 128), BF16),
            pltpu.VMEM((4, 4, 2, half, 128), F32),
            pltpu.VMEM((30, 2, rx + 16, 128), BF16),
            pltpu.VMEM((30, 2, rx + 16, 128), BF16),
            pltpu.VMEM((30, 2, ry + 16, 128), BF16),
            pltpu.VMEM((30, 2, ry + 16, 128), BF16),
            pltpu.VMEM((1, 8, half), F32),
            pltpu.VMEM((2, 8, half), F32),
            dma((10,)), dma((2,)), dma((2,)),
            dma((4, 4)), dma((4, 4)), dma((4, 4)), dma((4, 4)),
            dma((30,)), dma((30,)), dma((30,)), dma((30,)), dma, dma,
        ],
        compiler_params=pltpu.CompilerParams(
            collective_id=0, has_side_effects=True, vmem_limit_bytes=58 * 1024 * 1024),
        cost_estimate=pl.CostEstimate(flops=2 * tokens * wide * 2048, bytes_accessed=6 * 2**20, transcendentals=0),
    )(act, grad, q_in, q_out)
    return scores[:2].T


def solution(mesh):
    return jax.shard_map(
        scores_of,
        mesh=mesh,
        in_specs=(P("dp", "tensor"), P("dp", "tensor"), P("tensor", "dp"), P("tensor", "dp")),
        out_specs=P("dp", "tensor"),
        check_vma=False,
    )
```

```python
import functools
import math

import jax
import jax.numpy as jnp
from jax import lax
from jax.experimental import pallas as pl
from jax.experimental.pallas import tpu as pltpu
from jax.sharding import PartitionSpec as P

R = 32
MESH = pl.DeviceIdType.MESH
BF16, F32 = jnp.bfloat16, jnp.float32
SPAN, LOW = 250.0, -124.0
ORDER = (2, 1, 3, 0)
ROWS_X = 288
TASKS = (
    ('own', 0), ('xr', 1, 0), ('xr', 2, 0), ('own', 1), ('xr', 3, 0), ('own', 2), ('y', 0, 0, 0), ('own', 3),
    ('near', 0), ('y', 0, 1, 0), ('y', 0, 2, 0), ('y', 0, 3, 0), ('pn', 0), ('xr', 2, 3), ('xa', 3, 0),
    ('y', 0, 0, 3), ('xr', 2, 1), ('y', 1, 0, 0), ('y', 0, 0, 1), ('xa', 1, 0), ('near', 1), ('y', 1, 1, 0),
    ('pn', 1), ('xr', 1, 3), ('xa', 1, 3), ('y', 0, 1, 3), ('xr', 1, 1), ('y', 0, 1, 1), ('far', 0), ('y', 1, 3, 0),
    ('y', 1, 2, 0), ('xa', 1, 1), ('pf', 0), ('y', 0, 0, 2), ('y', 1, 0, 3), ('xr', 2, 2), ('xf', 0), ('ly', 0, 0),
    ('near', 2), ('y', 1, 0, 1), ('y', 2, 0, 0), ('pn', 2), ('far', 1), ('y', 0, 2, 1), ('xa', 3, 3), ('y', 0, 2, 3),
    ('xa', 3, 1), ('y', 2, 0, 3), ('pf', 1), ('y', 0, 1, 2), ('y', 1, 1, 1), ('xr', 1, 2), ('xr', 3, 1),
    ('y', 1, 1, 3), ('ly', 1, 0), ('xr', 3, 3), ('y', 2, 3, 0), ('y', 1, 0, 2), ('y', 2, 0, 1), ('y', 2, 1, 0),
    ('near', 3), ('y', 2, 2, 0), ('y', 1, 1, 2), ('pn', 3), ('far', 2), ('y', 0, 3, 1), ('y', 0, 3, 3),
    ('y', 2, 1, 3), ('y', 2, 1, 1), ('pf', 2), ('y', 0, 2, 2), ('xr', 3, 2), ('y', 1, 2, 1), ('y', 2, 0, 2),
    ('xa', 1, 2), ('far', 3), ('y', 1, 2, 3), ('xa', 3, 2), ('lx', 0), ('xf', 1), ('pf', 3), ('y', 0, 3, 2),
    ('ly', 0, 1), ('xf', 3), ('ly', 0, 3), ('y', 1, 2, 2), ('y', 2, 1, 2), ('lx', 2), ('ly', 2, 0), ('y', 1, 3, 3),
    ('y', 1, 3, 1), ('y', 2, 2, 1), ('y', 2, 2, 3), ('y', 1, 3, 2), ('lx', 1), ('xf', 2), ('ly', 0, 2), ('ly', 1, 1),
    ('ly', 1, 3), ('y', 2, 2, 2), ('lx', 5), ('lx', 4), ('y', 2, 3, 2), ('y', 2, 3, 3), ('y', 2, 3, 1), ('ly', 1, 2),
    ('ly', 2, 3), ('ly', 2, 1), ('lx', 9), ('ly', 2, 2),
)


def encode(value, box, top_box):
    rows = value.shape[0]
    size = jnp.abs(value).reshape(rows // 8, 8, 128)
    top = jnp.max(size, axis=0).astype(BF16).astype(F32)
    top_box[...] = top
    part = size * (1.0 / jnp.maximum(top, 1e-30))[None]
    root = part * lax.rsqrt(part + 1e-30)
    code = jnp.exp2(root * SPAN + LOW).reshape(rows, 128)
    box[...] = jnp.where(value < 0, -code, code).astype(BF16)


def decode(box, top):
    rows = box.shape[0]
    code = box[...].astype(F32)
    root = jnp.log(jnp.abs(code)) * (1.0 / (SPAN * math.log(2.0))) - LOW / SPAN
    size = ((root * root).reshape(rows // 8, 8, 128) * top[None]).reshape(rows, 128)
    return jnp.where(code < 0, -size, size)


def kernel(
    act, grad, q_in, q_out, out,
    a, q, part, sent_x, got_x, sent_y, got_y, tops, mine, theirs,
    load_sem, a_send, a_recv, z_send, z_recv, core_send, core_recv,
    send_x_sem, recv_x_sem, send_y_sem, recv_y_sem, end_send, end_recv,
):
    box_x, box_y = (sent_x, got_x, send_x_sem, recv_x_sem), (sent_y, got_y, send_y_sem, recv_y_sem)
    z, t = lax.axis_index("dp"), lax.axis_index("tensor")
    core, x, y = t % 2, (t // 2) % 4, t // 8
    tokens, w_in = act.shape
    w_out = grad.shape[1]
    half, wide = tokens // 2, w_in + w_out
    rx, ry = ROWS_X, half // 2 - ROWS_X

    def at(dx=0, dy=0, dz=0, other=False):
        index = (((y + dy + 4) % 4) * 4 + (x + dx + 4) % 4) * 2 + ((1 - core) if other else core)
        return ((z + dz + 4) % 4, index)

    own, partner_rows = core * half, (1 - core) * half

    loads = [
        pltpu.make_async_copy(act.at[pl.ds(own, half), :], a.at[:, pl.ds(0, w_in)], load_sem.at[0]),
        pltpu.make_async_copy(grad.at[pl.ds(own, half), :], a.at[:, pl.ds(w_in, w_out)], load_sem.at[1]),
    ]
    for j, step in enumerate(ORDER):
        columns = pl.ds(pl.multiple_of(((x + step) % 4) * 128, 128), 128)
        loads.append(pltpu.make_async_copy(q_in.at[:, columns], q.at[j, z, pl.ds(0, w_in), :], load_sem.at[2 + 2 * j]))
        loads.append(pltpu.make_async_copy(q_out.at[:, columns], q.at[j, z, pl.ds(w_in, w_out), :], load_sem.at[3 + 2 * j]))
    for load in loads:
        load.start()

    barrier = pltpu.get_barrier_semaphore()
    for device in (at(dx=1), at(dx=-1), at(dy=1), at(dy=-1), at(dz=1), at(dz=-1), at(other=True)):
        pl.semaphore_signal(barrier, inc=1, device_id=device, device_id_type=MESH)
    pl.semaphore_wait(barrier, 7)

    def copy(src, dst, send, recv, device):
        return pltpu.make_async_remote_copy(
            src_ref=src, dst_ref=dst, send_sem=send, recv_sem=recv, device_id=device, device_id_type=MESH)

    swaps = []
    for k, (low, count) in enumerate(((0, 2 * rx), (2 * rx, 2 * ry))):
        theirs_now = pl.ds(pl.multiple_of(partner_rows + low, 32), count)
        for h, (source, base, width) in enumerate(((act, wide, w_in), (grad, wide + w_in, w_out))):
            swaps.append(copy(source.at[theirs_now, :], a.at[pl.ds(low, count), pl.ds(base, width)],
                              a_send.at[2 * k + h], a_recv.at[2 * k + h], at(other=True)))

    def z_copy(j, kind):
        piece, low, count, dz = {
            0: (z, 0, wide, 1),
            1: (z, 0, wide, -1),
            2: ((z + 3) % 4, 0, wide // 2, 1),
            3: ((z + 1) % 4, wide // 2, wide // 2, -1),
        }[kind]
        ref = q.at[j, piece, pl.ds(low, count), :]
        return copy(ref, ref, z_send.at[j, kind], z_recv.at[j, kind], at(dz=dz))

    def z_arrival(j, kind):
        piece, low, count, dz = {
            0: ((z + 3) % 4, 0, wide, 1),
            1: ((z + 1) % 4, 0, wide, -1),
            2: ((z + 2) % 4, 0, wide // 2, 1),
            3: ((z + 2) % 4, wide // 2, wide // 2, -1),
        }[kind]
        ref = q.at[j, piece, pl.ds(low, count), :]
        return copy(ref, ref, z_send.at[j, kind], z_recv.at[j, kind], at(dz=dz))

    def core_copy(j, step):
        piece = (z + step) % 4
        return copy(q.at[j, piece, pl.ds(0, wide), :], q.at[j, piece, pl.ds(wide, wide), :],
                    core_send.at[j, step], core_recv.at[j, step], at(other=True))

    for j in range(4):
        loads[2 + 2 * j].wait()
        loads[3 + 2 * j].wait()
        if j < 2:
            z_copy(j, 0).start()
            z_copy(j, 1).start()
        core_copy(j, 0).start()
        if j == 0:
            swaps[0].start()
            swaps[1].start()
    swaps[2].start()
    swaps[3].start()

    def pass_near(j):
        z_arrival(j, 0).wait_recv()
        z_copy(j, 2).start()
        core_copy(j, 3).start()
        z_arrival(j, 1).wait_recv()
        z_copy(j, 3).start()
        core_copy(j, 1).start()
        if j < 2:
            z_copy(j + 2, 0).start()
            z_copy(j + 2, 1).start()

    def pass_far(j):
        z_arrival(j, 2).wait_recv()
        z_arrival(j, 3).wait_recv()
        core_copy(j, 2).start()

    def project(pieces, first, count_of):
        block = count_of // 2

        @pl.loop(0, 2)
        def _(i):
            line = pl.ds(pl.multiple_of(first + i * block, 32), block)
            for h, (low, count) in enumerate(((0, w_in), (w_in, w_out))):
                total = None
                for base in (low, low + wide):
                    right = [q[j, (z + step) % 4, pl.ds(base, count), :] for j, step in pieces]
                    right = right[0] if len(right) == 1 else jnp.concatenate(right, axis=1)
                    term = jnp.dot(a[line, pl.ds(base, count)], right, preferred_element_type=F32)
                    total = term if total is None else total + term
                for k, (j, step) in enumerate(pieces):
                    part[j, (z + step) % 4, h, line, :] = total[:, k * 128:(k + 1) * 128]

    def message(box, m, device):
        sent, got, out_sem, in_sem = box
        return copy(sent.at[m], got.at[m], out_sem.at[m], in_sem.at[m], device)

    def arrived(box, m):
        message(box, m, at(dx=1)).wait_recv()

    def read(box, m, h):
        got = box[1]
        r = (got.shape[1] - 16) // 2
        top = got[m, pl.ds(2 * r, 16), :].astype(F32).reshape(2, 8, 128)
        return decode(got.at[m, pl.ds(pl.multiple_of(h * r, 16), r), :], jnp.where(h == 0, top[0], top[1]))

    def send(box, m, source, device, add=None):
        sent = box[0]
        r = (sent.shape[1] - 16) // 2
        if add is not None:
            arrived(box, add)

        @pl.loop(0, 2)
        def _(h):
            value = source[h]
            if add is not None:
                value = value + read(box, add, h)
            encode(value, sent.at[m, pl.ds(pl.multiple_of(h * r, 16), r), :], tops.at[h])

        sent[m, pl.ds(2 * r, 16), :] = tops[...].reshape(16, 128).astype(BF16)
        message(box, m, device).start()

    def finish(box, target, first, second):
        arrived(box, first)
        arrived(box, second)

        @pl.loop(0, 2)
        def _(h):
            target[h] = target[h] + read(box, first, h) + read(box, second, h)

    def x_part(j, n, b):
        return part.at[j, n, :, pl.ds(pl.multiple_of(b * rx, 32), rx), :]

    def y_part(j, n, b):
        return part.at[j, n, :, pl.ds(pl.multiple_of(2 * rx + b * ry, 32), ry), :]

    def way_x(kind):
        return at(dx=jnp.where(kind < 3, 1, -1))

    def way_y(kind):
        return at(dy=jnp.where(kind < 3, 1, -1))

    def over_y(step, i, box, slot, source):
        n = (z + i) % 4
        role = (n - y + 4) % 4
        if step == 0:
            @pl.loop(0, jnp.where(role == 2, 2, jnp.where(role == 0, 0, 1)))
            def _(k):
                kind = jnp.where(role == 2, 3 * k, jnp.where(role == 1, 2, 5))
                b = jnp.where(role == 2, k, jnp.where(role == 1, 1, 0))
                send(box, slot(kind), source(n, b), way_y(kind))
        elif step == 1:
            @pl.when(role % 2 == 1)
            def _():
                kind = jnp.where(role == 1, 1, 4)
                send(box, slot(kind), source(n, role // 2), way_y(kind), add=slot(kind - 1))
        else:
            @pl.when(role == 0)
            def _():
                @pl.loop(0, 2)
                def _(b):
                    finish(box, source(n, b), slot(1 + 3 * b), slot(5 - 3 * b))

    here = set()

    def own_rows(k):
        if k not in here:
            here.add(k)
            if k == 0:
                loads[0].wait()
                loads[1].wait()
            swaps[2 * k].wait_recv()
            swaps[2 * k + 1].wait_recv()

    def pieces_at(pieces):
        for j, i in pieces:
            core_copy(j, i).wait_recv()
        return pieces

    def task(name, *index):
        k = index[0]
        if name == "near":
            pass_near(k)
        elif name == "far":
            pass_far(k)
        elif name == "own":
            pieces = [(2 * (k % 2), 0), (2 * (k % 2) + 1, 0)]
            own_rows(0)
            if k < 2:
                project(pieces_at(pieces), 0, 2 * rx)
            else:
                own_rows(1)
                project(pieces, 2 * rx, 2 * ry)
        elif name in ("pn", "pf"):
            own_rows(0)
            own_rows(1)
            project(pieces_at([(k, 3), (k, 1)] if name == "pn" else [(k, 2)]), 0, half)
        elif name == "xr":
            i = index[1]
            n = (z + i) % 4
            if k == 2:
                @pl.loop(0, 2)
                def _(b):
                    send(box_x, 12 * b + n, x_part(0, n, b), way_x(3 * b))
            elif k == 1:
                send(box_x, 8 + n, x_part(1, n, 1), right)
            else:
                send(box_x, 20 + n, x_part(2, n, 0), left)
        elif name == "xa":
            n = (z + index[1]) % 4
            if k == 1:
                send(box_x, 4 + n, x_part(1, n, 0), right, add=n)
            else:
                send(box_x, 16 + n, x_part(2, n, 1), left, add=12 + n)
        elif name == "xf":
            n = (z + k) % 4

            @pl.loop(0, 2)
            def _(b):
                finish(box_x, x_part(3, n, b), 4 + 12 * b + n, 20 - 12 * b + n)
        elif name == "y":
            j, i = index[1:]
            over_y(k, i, box_y, lambda kind: 4 * kind + j, lambda n, b: y_part(j, n, b))
        elif name == "ly":
            over_y(k, index[1], box_x, lambda kind: 24 + kind, lambda n, b: x_part(3, n, b))
        elif k == 0:
            @pl.loop(0, 2)
            def _(b):
                send(box_y, 24 + 3 * b, y_part(0, y, b), way_x(3 * b))
        elif k == 2:
            send(box_y, 26, y_part(1, y, 1), right)
        elif k == 5:
            send(box_y, 29, y_part(2, y, 0), left)
        elif k == 1:
            send(box_y, 25, y_part(1, y, 0), right, add=24)
        elif k == 4:
            send(box_y, 28, y_part(2, y, 1), left, add=27)
        else:
            @pl.loop(0, 2)
            def _(b):
                finish(box_y, y_part(3, y, b), 25 + 3 * b, 29 - 3 * b)

    right, left = at(dx=1), at(dx=-1)
    for name, *index in TASKS:
        task(name, *index)

    query = lax.broadcasted_iota(jnp.int32, (8, 128), 0)
    owner = lax.broadcasted_iota(jnp.int32, (8, 128), 1) // R

    def pick(which):
        return jnp.where((owner == query + 2 * which) & (query < 2), 1.0, 0.0).astype(BF16)

    rows = half // 4
    for g in range(4):
        line = pl.ds(g * rows, rows)
        product = part[3, y, 0, line, :] * part[3, y, 1, line, :] * (1.0 / math.sqrt(R))
        high = product.astype(BF16)
        rest = product - high.astype(F32)
        middle = rest.astype(BF16)
        low = (rest - middle.astype(F32)).astype(BF16)
        for which, target in ((core, mine), (1 - core, theirs)):
            mask = pick(which)
            total = None
            for term in (low, middle, high):
                s = lax.dot_general(mask, term, (((1,), (1,)), ((), ())), preferred_element_type=F32)
                total = s if total is None else total + s
            target[0, :, pl.ds(g * rows, rows)] = total
    final = copy(theirs.at[0], theirs.at[1], end_send, end_recv, at(other=True))
    final.start()
    out[:, pl.ds(pl.multiple_of(own, half), half)] = mine[0, pl.ds(0, 2), :]
    final.wait_recv()
    out[:, pl.ds(pl.multiple_of(partner_rows, half), half)] = theirs[1, pl.ds(0, 2), :]

    final.wait_send()
    for swap in swaps:
        swap.wait_send()
    for j in range(4):
        for k in range(4):
            z_copy(j, k).wait_send()
            core_copy(j, k).wait_send()

    @pl.loop(0, 30)
    def _(m):
        message(box_x, m, right).wait_send()
        message(box_y, m, right).wait_send()


def scores_of(act, grad, q_in, q_out):
    tokens, w_in = act.shape
    w_out = grad.shape[1]
    half, wide = tokens // 2, w_in + w_out
    rx, ry = ROWS_X, half // 2 - ROWS_X
    dma = pltpu.SemaphoreType.DMA
    scores = pl.pallas_call(
        kernel,
        out_shape=jax.ShapeDtypeStruct((2, tokens), F32),
        in_specs=[pl.BlockSpec(memory_space=pl.ANY)] * 4,
        out_specs=pl.BlockSpec(memory_space=pltpu.VMEM),
        scratch_shapes=[
            pltpu.VMEM((half, 2 * wide), BF16),
            pltpu.VMEM((4, 4, 2 * wide, 128), BF16),
            pltpu.VMEM((4, 4, 2, half, 128), F32),
            pltpu.VMEM((30, 2 * rx + 16, 128), BF16),
            pltpu.VMEM((30, 2 * rx + 16, 128), BF16),
            pltpu.VMEM((30, 2 * ry + 16, 128), BF16),
            pltpu.VMEM((30, 2 * ry + 16, 128), BF16),
            pltpu.VMEM((2, 8, 128), F32),
            pltpu.VMEM((1, 8, half), F32),
            pltpu.VMEM((2, 8, half), F32),
            dma((10,)), dma((4,)), dma((4,)),
            dma((4, 4)), dma((4, 4)), dma((4, 4)), dma((4, 4)),
            dma((30,)), dma((30,)), dma((30,)), dma((30,)), dma, dma,
        ],
        compiler_params=pltpu.CompilerParams(
            collective_id=0, has_side_effects=True, vmem_limit_bytes=58 * 1024 * 1024),
        cost_estimate=pl.CostEstimate(flops=2 * tokens * wide * 2048, bytes_accessed=6 * 2**20, transcendentals=0),
    )(act, grad, q_in, q_out)
    return scores.T


def solution(mesh):
    return jax.shard_map(
        scores_of,
        mesh=mesh,
        in_specs=(P("dp", "tensor"), P("dp", "tensor"), P("tensor", "dp"), P("tensor", "dp")),
        out_specs=P("dp", "tensor"),
        check_vma=False,
    )
```

```python
import functools
import math

import jax
import jax.numpy as jnp
from jax import lax
from jax.experimental import pallas as pl
from jax.experimental.pallas import tpu as pltpu
from jax.sharding import PartitionSpec as P

R = 32
MESH = pl.DeviceIdType.MESH
BF16, F32 = jnp.bfloat16, jnp.float32
SPAN, LOW = 250.0, -124.0
ORDER = (2, 1, 3, 0)
ROWS_X = (320, 224, 352, 224)
CUTS = 2
TASKS = (
    ('own', 0), ('own', 1), ('z', 1), ('xr', 2, 0), ('own', 3), ('own', 2), ('y', 0, 1, 0), ('near', 0),
    ('y', 0, 2, 0), ('xr', 3, 0), ('xr', 1, 0), ('pass', 0), ('pn', 0), ('y', 0, 0, 1), ('y', 0, 0, 3), ('xr', 2, 1),
    ('near', 1), ('z', 2), ('xa', 3, 0), ('xr', 2, 3), ('xa', 1, 0), ('pn', 1), ('y', 0, 1, 1), ('y', 0, 1, 3),
    ('y', 1, 1, 0), ('far', 0), ('pf', 0), ('pass', 1), ('y', 1, 2, 0), ('y', 0, 0, 2), ('y', 1, 0, 3),
    ('y', 0, 0, 0), ('xr', 2, 2), ('y', 1, 0, 1), ('near', 2), ('xa', 1, 1), ('pass', 2), ('z', 3), ('y', 1, 1, 3),
    ('y', 1, 0, 2), ('xa', 1, 3), ('y', 1, 1, 1), ('pn', 2), ('xr', 3, 3), ('xf', 0), ('xr', 3, 1), ('y', 0, 3, 0),
    ('y', 0, 2, 3), ('xr', 1, 1), ('y', 0, 2, 1), ('far', 1), ('far', 2), ('y', 2, 0, 3), ('xa', 3, 1), ('pf', 1),
    ('y', 2, 2, 0), ('xa', 3, 3), ('y', 0, 1, 2), ('xr', 1, 2), ('y', 1, 0, 0), ('pf', 2), ('y', 0, 2, 2),
    ('y', 1, 2, 1), ('ly', 0, 0, 1), ('y', 2, 0, 1), ('xr', 1, 3), ('y', 2, 0, 2), ('near', 3), ('y', 1, 1, 2),
    ('y', 1, 2, 3), ('xa', 3, 2), ('pass', 3), ('y', 1, 3, 0), ('y', 2, 0, 0), ('xa', 1, 2), ('y', 1, 2, 2),
    ('pn', 3), ('y', 0, 3, 1), ('y', 0, 3, 3), ('xr', 3, 2), ('lx', 0), ('xf', 1), ('ly', 0, 1, 1), ('far', 3),
    ('xf', 3), ('ly', 0, 3, 0), ('ly', 0, 1, 0), ('y', 2, 2, 1), ('ly', 0, 3, 1), ('ly', 0, 0, 0), ('y', 2, 2, 2),
    ('pf', 3), ('y', 2, 1, 2), ('y', 2, 1, 0), ('y', 0, 3, 2), ('y', 2, 1, 3), ('ly', 1, 1, 1), ('y', 2, 1, 1),
    ('ly', 1, 3, 1), ('xf', 2), ('ly', 0, 2, 0), ('ly', 0, 2, 1), ('y', 1, 3, 1), ('ly', 1, 0, 1), ('y', 2, 2, 3),
    ('y', 1, 3, 2), ('lx', 4), ('y', 1, 3, 3), ('lx', 2), ('ly', 1, 0, 0), ('y', 2, 3, 0), ('ly', 2, 3, 1), ('lx', 1),
    ('ly', 1, 1, 0), ('ly', 1, 2, 0), ('ly', 1, 3, 0), ('lx', 5), ('ly', 1, 2, 1), ('ly', 2, 0, 0), ('ly', 2, 0, 1),
    ('y', 2, 3, 1), ('ly', 2, 2, 0), ('ly', 2, 1, 1), ('y', 2, 3, 3), ('y', 2, 3, 2), ('lx', 9), ('ly', 2, 1, 0),
    ('ly', 2, 3, 0), ('ly', 2, 2, 1),
)


def encode(value, box, top_box):
    rows = value.shape[0]
    size = jnp.abs(value).reshape(rows // 8, 8, 128)
    top = jnp.max(size, axis=0).astype(BF16).astype(F32)
    top_box[...] = top
    part = size * (1.0 / jnp.maximum(top, 1e-30))[None]
    root = part * lax.rsqrt(part + 1e-30)
    code = jnp.exp2(root * SPAN + LOW).reshape(rows, 128)
    box[...] = jnp.where(value < 0, -code, code).astype(BF16)


def decode(box, top):
    rows = box.shape[0]
    code = box[...].astype(F32)
    root = jnp.log(jnp.abs(code)) * (1.0 / (SPAN * math.log(2.0))) - LOW / SPAN
    size = ((root * root).reshape(rows // 8, 8, 128) * top[None]).reshape(rows, 128)
    return jnp.where(code < 0, -size, size)


def kernel(
    act, grad, q_in, q_out, out,
    a, q, part, sent_x, got_x, sent_y, got_y, tops, mine, theirs,
    load_sem, a_send, a_recv, z_send, z_recv, core_send, core_recv,
    send_x_sem, recv_x_sem, send_y_sem, recv_y_sem, end_send, end_recv,
):
    box_x, box_y = (sent_x, got_x, send_x_sem, recv_x_sem), (sent_y, got_y, send_y_sem, recv_y_sem)
    z, t = lax.axis_index("dp"), lax.axis_index("tensor")
    core, x, y = t % 2, (t // 2) % 4, t // 8
    tokens, w_in = act.shape
    w_out = grad.shape[1]
    half, wide = tokens // 2, w_in + w_out
    rows_x = ROWS_X
    rows_y = tuple(half // 2 - r for r in ROWS_X)

    def at(dx=0, dy=0, dz=0, other=False):
        index = (((y + dy + 4) % 4) * 4 + (x + dx + 4) % 4) * 2 + ((1 - core) if other else core)
        return ((z + dz + 4) % 4, index)

    own, partner_rows = core * half, (1 - core) * half

    barrier = pltpu.get_barrier_semaphore()
    for device in (at(dx=1), at(dx=-1), at(dy=1), at(dy=-1), at(dz=1), at(dz=-1), at(other=True)):
        pl.semaphore_signal(barrier, inc=1, device_id=device, device_id_type=MESH)

    loads = [
        pltpu.make_async_copy(act.at[pl.ds(own, half), :], a.at[:, pl.ds(0, w_in)], load_sem.at[0]),
        pltpu.make_async_copy(grad.at[pl.ds(own, half), :], a.at[:, pl.ds(w_in, w_out)], load_sem.at[1]),
    ]
    for j, step in enumerate(ORDER):
        columns = pl.ds(pl.multiple_of(((x + step) % 4) * 128, 128), 128)
        loads.append(pltpu.make_async_copy(q_in.at[:, columns], q.at[j, z, pl.ds(0, w_in), :], load_sem.at[2 + 2 * j]))
        loads.append(pltpu.make_async_copy(q_out.at[:, columns], q.at[j, z, pl.ds(w_in, w_out), :], load_sem.at[3 + 2 * j]))
    for load in loads:
        load.start()

    pl.semaphore_wait(barrier, 7)

    def copy(src, dst, send, recv, device):
        return pltpu.make_async_remote_copy(
            src_ref=src, dst_ref=dst, send_sem=send, recv_sem=recv, device_id=device, device_id_type=MESH)

    swaps = []
    for k, (low, count) in enumerate(((0, 2 * rows_x[0]), (2 * rows_x[0], 2 * rows_y[0]))):
        theirs_now = pl.ds(pl.multiple_of(partner_rows + low, 32), count)
        for h, (source, base, width) in enumerate(((act, wide, w_in), (grad, wide + w_in, w_out))):
            swaps.append(copy(source.at[theirs_now, :], a.at[pl.ds(low, count), pl.ds(base, width)],
                              a_send.at[2 * k + h], a_recv.at[2 * k + h], at(other=True)))

    def z_copy(j, kind):
        piece, low, count, dz = {
            0: (z, 0, wide, 1),
            1: (z, 0, wide, -1),
            2: ((z + 3) % 4, 0, wide // 2, 1),
            3: ((z + 1) % 4, wide // 2, wide // 2, -1),
        }[kind]
        ref = q.at[j, piece, pl.ds(low, count), :]
        return copy(ref, ref, z_send.at[j, kind], z_recv.at[j, kind], at(dz=dz))

    def z_arrival(j, kind):
        piece, low, count, dz = {
            0: ((z + 3) % 4, 0, wide, 1),
            1: ((z + 1) % 4, 0, wide, -1),
            2: ((z + 2) % 4, 0, wide // 2, 1),
            3: ((z + 2) % 4, wide // 2, wide // 2, -1),
        }[kind]
        ref = q.at[j, piece, pl.ds(low, count), :]
        return copy(ref, ref, z_send.at[j, kind], z_recv.at[j, kind], at(dz=dz))

    def core_copy(j, step):
        piece = (z + step) % 4
        return copy(q.at[j, piece, pl.ds(0, wide), :], q.at[j, piece, pl.ds(wide, wide), :],
                    core_send.at[j, step], core_recv.at[j, step], at(other=True))

    for j in range(4):
        loads[2 + 2 * j].wait()
        loads[3 + 2 * j].wait()
        if j == 0:
            z_copy(j, 0).start()
            z_copy(j, 1).start()
        core_copy(j, 0).start()
        if j == 0:
            swaps[0].start()
            swaps[1].start()
    swaps[2].start()
    swaps[3].start()

    here = set()

    def near_here(j):
        if j not in here:
            here.add(j)
            z_arrival(j, 0).wait_recv()
            z_arrival(j, 1).wait_recv()

    def project(pieces, first, count_of):
        block = count_of // 2

        @pl.loop(0, 2)
        def _(i):
            line = pl.ds(pl.multiple_of(first + i * block, 32), block)
            for h, (low, count) in enumerate(((0, w_in), (w_in, w_out))):
                total = None
                for base in (low, low + wide):
                    right = [q[j, (z + step) % 4, pl.ds(base, count), :] for j, step in pieces]
                    right = right[0] if len(right) == 1 else jnp.concatenate(right, axis=1)
                    term = jnp.dot(a[line, pl.ds(base, count)], right, preferred_element_type=F32)
                    total = term if total is None else total + term
                for k, (j, step) in enumerate(pieces):
                    part[j, (z + step) % 4, h, line, :] = total[:, k * 128:(k + 1) * 128]

    def message(box, m, device, r):
        sent, got, out_sem, in_sem = box
        line = pl.ds(0, 2 * r + 16)
        return copy(sent.at[m, line, :], got.at[m, line, :], out_sem.at[m], in_sem.at[m], device)

    def arrived(box, m, r):
        message(box, m, at(dx=1), r).wait_recv()

    def left_box(box, m, r):
        message(box, m, at(dx=1), r).wait_send()

    def read(box, m, h, r):
        got = box[1]
        top = got[m, pl.ds(2 * r, 16), :].astype(F32).reshape(2, 8, 128)
        return decode(got.at[m, pl.ds(pl.multiple_of(h * r, 16), r), :], jnp.where(h == 0, top[0], top[1]))

    def send(box, m, source, device, add=None):
        sent, r = box[0], source.shape[1]
        if add is not None:
            arrived(box, add, r)

        @pl.loop(0, 2)
        def _(h):
            value = source[h]
            if add is not None:
                value = value + read(box, add, h, r)
            encode(value, sent.at[m, pl.ds(pl.multiple_of(h * r, 16), r), :], tops.at[h])

        sent[m, pl.ds(2 * r, 16), :] = tops[...].reshape(16, 128).astype(BF16)
        message(box, m, device, r).start()

    def finish(box, target, first, second):
        r = target.shape[1]
        arrived(box, first, r)
        arrived(box, second, r)

        @pl.loop(0, 2)
        def _(h):
            target[h] = target[h] + read(box, first, h, r) + read(box, second, h, r)

    def x_part(j, i, b, c=0, cuts=1):
        r = rows_x[i]
        return part.at[j, (z + i) % 4, :, pl.ds(pl.multiple_of(b * r + c * (r // cuts), 16), r // cuts), :]

    def y_part(j, i, b):
        r = rows_y[i]
        return part.at[j, (z + i) % 4, :, pl.ds(pl.multiple_of(2 * rows_x[i] + b * r, 16), r), :]

    def way_x(kind):
        return at(dx=jnp.where(kind < 3, 1, -1))

    def way_y(kind):
        return at(dy=jnp.where(kind < 3, 1, -1))

    def over_y(step, i, box, slot, source):
        role = (z + i - y + 4) % 4
        if step == 0:
            @pl.loop(0, jnp.where(role == 2, 2, jnp.where(role == 0, 0, 1)))
            def _(k):
                kind = jnp.where(role == 2, 3 * k, jnp.where(role == 1, 2, 5))
                b = jnp.where(role == 2, k, jnp.where(role == 1, 1, 0))
                send(box, slot(kind), source(b), way_y(kind))
        elif step == 1:
            @pl.when(role % 2 == 1)
            def _():
                kind = jnp.where(role == 1, 1, 4)
                send(box, slot(kind), source(role // 2), way_y(kind), add=slot(kind - 1))
        else:
            @pl.when(role == 0)
            def _():
                @pl.loop(0, 2)
                def _(b):
                    finish(box, source(b), slot(1 + 3 * b), slot(5 - 3 * b))

    def over_y_left(i, box, slot, r):
        role = (z + i - y + 4) % 4

        @pl.when(role == 2)
        def _():
            left_box(box, slot(0), r)
            left_box(box, slot(3), r)

        @pl.when(role % 2 == 1)
        def _():
            kind = jnp.where(role == 1, 1, 4)
            left_box(box, slot(kind), r)
            left_box(box, slot(kind + 1), r)

    def own_place(body):
        for i in range(4):
            @pl.when((y - z + 4) % 4 == i)
            def _(i=i):
                body(i)

    def own_rows(k):
        if ("rows", k) not in here:
            here.add(("rows", k))
            if k == 0:
                loads[0].wait()
                loads[1].wait()
            swaps[2 * k].wait_recv()
            swaps[2 * k + 1].wait_recv()

    def pieces_at(pieces):
        for j, i in pieces:
            core_copy(j, i).wait_recv()
        return pieces

    def last_x(k, i):
        if k == 0:
            @pl.loop(0, 2)
            def _(b):
                send(box_y, 24 + 3 * b, y_part(0, i, b), way_x(3 * b))
        elif k == 2:
            send(box_y, 26, y_part(1, i, 1), right)
        elif k == 5:
            send(box_y, 29, y_part(2, i, 0), left)
        elif k == 1:
            send(box_y, 25, y_part(1, i, 0), right, add=24)
        elif k == 4:
            send(box_y, 28, y_part(2, i, 1), left, add=27)
        else:
            @pl.loop(0, 2)
            def _(b):
                finish(box_y, y_part(3, i, b), 25 + 3 * b, 29 - 3 * b)

    def task(name, *index):
        k = index[0]
        if name == "z":
            if k >= 2:
                near_here(k - 2)
            z_copy(k, 0).start()
            z_copy(k, 1).start()
        elif name == "pass":
            near_here(k)
            z_copy(k, 2).start()
            z_copy(k, 3).start()
        elif name == "near":
            near_here(k)
            core_copy(k, 3).start()
            core_copy(k, 1).start()
        elif name == "far":
            z_arrival(k, 2).wait_recv()
            z_arrival(k, 3).wait_recv()
            core_copy(k, 2).start()
        elif name == "own":
            pieces = [(2 * (k % 2), 0), (2 * (k % 2) + 1, 0)]
            own_rows(0)
            if k < 2:
                project(pieces_at(pieces), 0, 2 * rows_x[0])
            else:
                own_rows(1)
                project(pieces, 2 * rows_x[0], 2 * rows_y[0])
        elif name in ("pn", "pf"):
            own_rows(0)
            own_rows(1)
            project(pieces_at([(k, 3), (k, 1)] if name == "pn" else [(k, 2)]), 0, half)
        elif name == "xr":
            i = index[1]
            n = (z + i) % 4
            if k == 2:
                @pl.loop(0, 2)
                def _(b):
                    send(box_x, 12 * b + n, x_part(0, i, b), way_x(3 * b))
            elif k == 1:
                send(box_x, 8 + n, x_part(1, i, 1), right)
            else:
                send(box_x, 20 + n, x_part(2, i, 0), left)
        elif name == "xa":
            i = index[1]
            n = (z + i) % 4
            if k == 1:
                send(box_x, 4 + n, x_part(1, i, 0), right, add=n)
            else:
                send(box_x, 16 + n, x_part(2, i, 1), left, add=12 + n)
        elif name == "xf":
            n = (z + k) % 4

            @pl.loop(0, 2)
            def _(b):
                finish(box_x, x_part(3, k, b), 4 + 12 * b + n, 20 - 12 * b + n)
        elif name == "y":
            j, i = index[1:]
            over_y(k, i, box_y, lambda kind: 4 * kind + j, lambda b: y_part(j, i, b))
        elif name == "ly":
            i, c = index[1:]
            over_y(k, i, box_x, lambda kind: 24 + 6 * c + kind, lambda b: x_part(3, i, b, c, CUTS))
        else:
            own_place(functools.partial(last_x, k))

    right, left = at(dx=1), at(dx=-1)
    for name, *index in TASKS:
        task(name, *index)

    query = lax.broadcasted_iota(jnp.int32, (8, 128), 0)
    owner = lax.broadcasted_iota(jnp.int32, (8, 128), 1) // R

    mask = jnp.concatenate([
        jnp.where((owner == query + 2 * which) & (query < 2), 1.0, 0.0).astype(BF16) for which in (core, 1 - core)], axis=0)
    rows = half // 4
    for g in range(4):
        line = pl.ds(g * rows, rows)
        product = part[3, y, 0, line, :] * part[3, y, 1, line, :] * (1.0 / math.sqrt(R))
        high = product.astype(BF16)
        rest = product - high.astype(F32)
        middle = rest.astype(BF16)
        low = (rest - middle.astype(F32)).astype(BF16)
        total = None
        for term in (low, middle, high):
            s = lax.dot_general(mask, term, (((1,), (1,)), ((), ())), preferred_element_type=F32)
            total = s if total is None else total + s
        mine[0, :, line] = total[:8]
        theirs[0, :, line] = total[8:]
    final = copy(theirs.at[0], theirs.at[1], end_send, end_recv, at(other=True))
    final.start()
    out[:, pl.ds(pl.multiple_of(own, half), half)] = mine[0, pl.ds(0, 2), :]
    final.wait_recv()
    out[:, pl.ds(pl.multiple_of(partner_rows, half), half)] = theirs[1, pl.ds(0, 2), :]

    final.wait_send()
    for swap in swaps:
        swap.wait_send()
    for j in range(4):
        for k in range(4):
            z_copy(j, k).wait_send()
            core_copy(j, k).wait_send()

    for i in range(4):
        @pl.loop(0, 6)
        def _(kind):
            left_box(box_x, kind * 4 + (z + i) % 4, rows_x[i])

        @pl.loop(0, 4)
        def _(j):
            over_y_left(i, box_y, lambda kind: 4 * kind + j, rows_y[i])

        for c in range(CUTS):
            over_y_left(i, box_x, lambda kind: 24 + 6 * c + kind, rows_x[i] // CUTS)

    def last_left(i):
        @pl.loop(0, 6)
        def _(kind):
            left_box(box_y, 24 + kind, rows_y[i])

    own_place(last_left)


def scores_of(act, grad, q_in, q_out):
    tokens, w_in = act.shape
    w_out = grad.shape[1]
    half, wide = tokens // 2, w_in + w_out
    rx, ry = max(ROWS_X), half // 2 - min(ROWS_X)
    slots = 24 + 6 * CUTS
    dma = pltpu.SemaphoreType.DMA
    scores = pl.pallas_call(
        kernel,
        out_shape=jax.ShapeDtypeStruct((2, tokens), F32),
        in_specs=[pl.BlockSpec(memory_space=pl.ANY)] * 4,
        out_specs=pl.BlockSpec(memory_space=pltpu.VMEM),
        scratch_shapes=[
            pltpu.VMEM((half, 2 * wide), BF16),
            pltpu.VMEM((4, 4, 2 * wide, 128), BF16),
            pltpu.VMEM((4, 4, 2, half, 128), F32),
            pltpu.VMEM((slots, 2 * rx + 16, 128), BF16),
            pltpu.VMEM((slots, 2 * rx + 16, 128), BF16),
            pltpu.VMEM((30, 2 * ry + 16, 128), BF16),
            pltpu.VMEM((30, 2 * ry + 16, 128), BF16),
            pltpu.VMEM((2, 8, 128), F32),
            pltpu.VMEM((1, 8, half), F32),
            pltpu.VMEM((2, 8, half), F32),
            dma((10,)), dma((4,)), dma((4,)),
            dma((4, 4)), dma((4, 4)), dma((4, 4)), dma((4, 4)),
            dma((slots,)), dma((slots,)), dma((30,)), dma((30,)), dma, dma,
        ],
        compiler_params=pltpu.CompilerParams(
            collective_id=0, has_side_effects=True, vmem_limit_bytes=58 * 1024 * 1024),
        cost_estimate=pl.CostEstimate(flops=2 * tokens * wide * 2048, bytes_accessed=6 * 2**20, transcendentals=0),
    )(act, grad, q_in, q_out)
    return scores.T


def solution(mesh):
    return jax.shard_map(
        scores_of,
        mesh=mesh,
        in_specs=(P("dp", "tensor"), P("dp", "tensor"), P("tensor", "dp"), P("tensor", "dp")),
        out_specs=P("dp", "tensor"),
        check_vma=False,
    )
```

```python
import functools
import math

import jax
import jax.numpy as jnp
from jax import lax
from jax.experimental import pallas as pl
from jax.experimental.pallas import tpu as pltpu
from jax.sharding import PartitionSpec as P

R = 32
MESH = pl.DeviceIdType.MESH
BF16, F32 = jnp.bfloat16, jnp.float32
SPAN, LOW = 250.0, -124.0
ORDER = (2, 1, 3, 0)
ROWS_X = (320, 224, 352, 224)
CUTS = 1
TASKS = (
    ('own', 0), ('xr', 2, 0), ('z', 1), ('own', 1), ('own', 2), ('near', 0), ('y', 0, 1, 0), ('y', 0, 0, 0),
    ('xr', 1, 0), ('pass', 0), ('pn', 0), ('xa', 3, 0), ('xa', 1, 0), ('y', 0, 0, 3), ('xr', 3, 0), ('y', 0, 0, 1),
    ('near', 1), ('z', 2), ('pass', 1), ('xr', 2, 3), ('pn', 1), ('y', 0, 1, 1), ('y', 0, 1, 3), ('y', 1, 1, 0),
    ('far', 0), ('xr', 2, 1), ('y', 1, 0, 1), ('own', 3), ('xr', 1, 1), ('xr', 1, 3), ('y', 1, 0, 3), ('xf', 0),
    ('pf', 0), ('y', 0, 0, 2), ('y', 0, 2, 0), ('near', 2), ('pass', 2), ('y', 1, 1, 3), ('xa', 1, 1), ('xr', 2, 2),
    ('y', 1, 1, 1), ('z', 3), ('pn', 2), ('y', 0, 2, 3), ('y', 0, 2, 1), ('far', 1), ('xr', 3, 1), ('xa', 3, 1),
    ('y', 2, 0, 3), ('y', 1, 0, 0), ('y', 1, 0, 2), ('far', 2), ('pf', 1), ('y', 0, 1, 2), ('pf', 2), ('y', 0, 2, 2),
    ('xr', 3, 2), ('ly', 0, 0, 0), ('y', 2, 0, 1), ('xr', 1, 2), ('y', 1, 2, 3), ('y', 0, 3, 0), ('y', 1, 2, 1),
    ('xa', 3, 2), ('pass', 3), ('near', 3), ('y', 1, 1, 2), ('y', 1, 2, 0), ('xa', 3, 3), ('xa', 1, 2),
    ('y', 2, 0, 0), ('y', 1, 2, 2), ('pn', 3), ('y', 0, 3, 3), ('y', 0, 3, 1), ('far', 3), ('y', 2, 1, 1),
    ('y', 2, 1, 2), ('xa', 1, 3), ('xr', 3, 3), ('y', 2, 1, 3), ('pf', 3), ('y', 0, 3, 2), ('xf', 1), ('xf', 2),
    ('ly', 0, 2, 0), ('y', 2, 1, 0), ('y', 2, 2, 2), ('y', 2, 0, 2), ('ly', 1, 0, 0), ('y', 2, 2, 1), ('lx', 0),
    ('y', 1, 3, 1), ('y', 1, 3, 3), ('lx', 2), ('y', 2, 2, 0), ('y', 2, 2, 3), ('ly', 0, 1, 0), ('lx', 5), ('xf', 3),
    ('ly', 0, 3, 0), ('y', 1, 3, 2), ('lx', 4), ('lx', 1), ('ly', 1, 3, 0), ('y', 1, 3, 0), ('ly', 2, 0, 0),
    ('ly', 1, 2, 0), ('ly', 1, 1, 0), ('left', 0), ('y', 2, 3, 3), ('y', 2, 3, 0), ('y', 2, 3, 2), ('y', 2, 3, 1),
    ('lx', 9), ('ly', 2, 2, 0), ('ly', 2, 1, 0), ('ly', 2, 3, 0),
)


def encode(value, box, top_box):
    rows = value.shape[0]
    size = jnp.abs(value).reshape(rows // 8, 8, 128)
    top = jnp.max(size, axis=0).astype(BF16).astype(F32)
    top_box[...] = top
    part = size * (SPAN * SPAN / jnp.maximum(top, 1e-30))[None]
    root = part * lax.rsqrt(part + 1e-30)
    code = jnp.exp2(root + LOW).reshape(rows, 128)
    box[...] = jnp.where(value < 0, -code, code).astype(BF16)


def decode(box, top):
    rows = box.shape[0]
    code = box[...].astype(F32)
    root = jnp.log(jnp.abs(code)) * (1.0 / (SPAN * math.log(2.0))) - LOW / SPAN
    size = ((root * root).reshape(rows // 8, 8, 128) * top[None]).reshape(rows, 128)
    return jnp.where(code < 0, -size, size)


def kernel(
    act, grad, q_in, q_out, out,
    a, q, part, sent_x, got_x, sent_y, got_y, tops, mine, theirs,
    load_sem, a_send, a_recv, z_send, z_recv, core_send, core_recv,
    send_x_sem, recv_x_sem, send_y_sem, recv_y_sem, end_send, end_recv,
):
    box_x, box_y = (sent_x, got_x, send_x_sem, recv_x_sem), (sent_y, got_y, send_y_sem, recv_y_sem)
    z, t = lax.axis_index("dp"), lax.axis_index("tensor")
    core, x, y = t % 2, (t // 2) % 4, t // 8
    tokens, w_in = act.shape
    w_out = grad.shape[1]
    half, wide = tokens // 2, w_in + w_out
    rows_x = ROWS_X
    rows_y = tuple(half // 2 - r for r in ROWS_X)

    def at(dx=0, dy=0, dz=0, other=False):
        index = (((y + dy + 4) % 4) * 4 + (x + dx + 4) % 4) * 2 + ((1 - core) if other else core)
        return ((z + dz + 4) % 4, index)

    own, partner_rows = core * half, (1 - core) * half

    barrier = pltpu.get_barrier_semaphore()
    for device in (at(dx=1), at(dx=-1), at(dy=1), at(dy=-1), at(dz=1), at(dz=-1), at(other=True)):
        pl.semaphore_signal(barrier, inc=1, device_id=device, device_id_type=MESH)

    loads = [
        pltpu.make_async_copy(act.at[pl.ds(own, half), :], a.at[:, pl.ds(0, w_in)], load_sem.at[0]),
        pltpu.make_async_copy(grad.at[pl.ds(own, half), :], a.at[:, pl.ds(w_in, w_out)], load_sem.at[1]),
    ]
    for j, step in enumerate(ORDER):
        columns = pl.ds(pl.multiple_of(((x + step) % 4) * 128, 128), 128)
        loads.append(pltpu.make_async_copy(q_in.at[:, columns], q.at[j, z, pl.ds(0, w_in), :], load_sem.at[2 + 2 * j]))
        loads.append(pltpu.make_async_copy(q_out.at[:, columns], q.at[j, z, pl.ds(w_in, w_out), :], load_sem.at[3 + 2 * j]))
    for load in loads:
        load.start()

    pl.semaphore_wait(barrier, 7)

    def copy(src, dst, send, recv, device):
        return pltpu.make_async_remote_copy(
            src_ref=src, dst_ref=dst, send_sem=send, recv_sem=recv, device_id=device, device_id_type=MESH)

    swaps = []
    for k, (low, count) in enumerate(((0, 2 * rows_x[0]), (2 * rows_x[0], 2 * rows_y[0]))):
        theirs_now = pl.ds(pl.multiple_of(partner_rows + low, 32), count)
        for h, (source, base, width) in enumerate(((act, wide, w_in), (grad, wide + w_in, w_out))):
            swaps.append(copy(source.at[theirs_now, :], a.at[pl.ds(low, count), pl.ds(base, width)],
                              a_send.at[2 * k + h], a_recv.at[2 * k + h], at(other=True)))

    def z_copy(j, kind):
        piece, low, count, dz = {
            0: (z, 0, wide, 1),
            1: (z, 0, wide, -1),
            2: ((z + 3) % 4, 0, wide // 2, 1),
            3: ((z + 1) % 4, wide // 2, wide // 2, -1),
        }[kind]
        ref = q.at[j, piece, pl.ds(low, count), :]
        return copy(ref, ref, z_send.at[j, kind], z_recv.at[j, kind], at(dz=dz))

    def z_arrival(j, kind):
        piece, low, count, dz = {
            0: ((z + 3) % 4, 0, wide, 1),
            1: ((z + 1) % 4, 0, wide, -1),
            2: ((z + 2) % 4, 0, wide // 2, 1),
            3: ((z + 2) % 4, wide // 2, wide // 2, -1),
        }[kind]
        ref = q.at[j, piece, pl.ds(low, count), :]
        return copy(ref, ref, z_send.at[j, kind], z_recv.at[j, kind], at(dz=dz))

    def core_copy(j, step):
        piece = (z + step) % 4
        return copy(q.at[j, piece, pl.ds(0, wide), :], q.at[j, piece, pl.ds(wide, wide), :],
                    core_send.at[j, step], core_recv.at[j, step], at(other=True))

    for j in range(4):
        loads[2 + 2 * j].wait()
        loads[3 + 2 * j].wait()
        if j == 0:
            z_copy(j, 0).start()
            z_copy(j, 1).start()
        core_copy(j, 0).start()
        if j == 0:
            swaps[0].start()
            swaps[1].start()
    swaps[2].start()
    swaps[3].start()

    here = set()

    def near_here(j):
        if j not in here:
            here.add(j)
            z_arrival(j, 0).wait_recv()
            z_arrival(j, 1).wait_recv()

    def project(pieces, first, count_of):
        block = count_of // 2

        @pl.loop(0, 2)
        def _(i):
            line = pl.ds(pl.multiple_of(first + i * block, 32), block)
            for h, (low, count) in enumerate(((0, w_in), (w_in, w_out))):
                bases = (low, low + wide)
                rows_of = jnp.concatenate([a[line, pl.ds(base, count)] for base in bases], axis=1)
                columns = [
                    jnp.concatenate([q[j, (z + step) % 4, pl.ds(base, count), :] for base in bases], axis=0) for j, step in pieces]
                columns = columns[0] if len(columns) == 1 else jnp.concatenate(columns, axis=1)
                total = jnp.dot(rows_of, columns, preferred_element_type=F32)
                for k, (j, step) in enumerate(pieces):
                    part[j, (z + step) % 4, h, line, :] = total[:, k * 128:(k + 1) * 128]

    def message(box, m, device, r):
        sent, got, out_sem, in_sem = box
        line = pl.ds(0, 2 * r + 16)
        return copy(sent.at[m, line, :], got.at[m, line, :], out_sem.at[m], in_sem.at[m], device)

    def arrived(box, m, r):
        message(box, m, at(dx=1), r).wait_recv()

    def left_box(box, m, r):
        message(box, m, at(dx=1), r).wait_send()

    def read(box, m, h, r):
        got = box[1]
        top = got[m, pl.ds(2 * r, 16), :].astype(F32).reshape(2, 8, 128)
        return decode(got.at[m, pl.ds(pl.multiple_of(h * r, 16), r), :], jnp.where(h == 0, top[0], top[1]))

    def send(box, m, source, device, add=None):
        sent, r = box[0], source.shape[1]
        if add is not None:
            arrived(box, add, r)

        @pl.loop(0, 2)
        def _(h):
            value = source[h]
            if add is not None:
                value = value + read(box, add, h, r)
            encode(value, sent.at[m, pl.ds(pl.multiple_of(h * r, 16), r), :], tops.at[h])

        sent[m, pl.ds(2 * r, 16), :] = tops[...].reshape(16, 128).astype(BF16)
        message(box, m, device, r).start()

    def finish(box, target, first, second):
        r = target.shape[1]
        arrived(box, first, r)
        arrived(box, second, r)

        @pl.loop(0, 2)
        def _(h):
            target[h] = target[h] + read(box, first, h, r) + read(box, second, h, r)

    def x_part(j, i, b, c=0, cuts=1):
        r = rows_x[i]
        return part.at[j, (z + i) % 4, :, pl.ds(pl.multiple_of(b * r + c * (r // cuts), 16), r // cuts), :]

    def y_part(j, i, b):
        r = rows_y[i]
        return part.at[j, (z + i) % 4, :, pl.ds(pl.multiple_of(2 * rows_x[i] + b * r, 16), r), :]

    def way_x(kind):
        return at(dx=jnp.where(kind < 3, 1, -1))

    def way_y(kind):
        return at(dy=jnp.where(kind < 3, 1, -1))

    def over_y(step, i, box, slot, source):
        role = (z + i - y + 4) % 4
        if step == 0:
            @pl.loop(0, jnp.where(role == 2, 2, jnp.where(role == 0, 0, 1)))
            def _(k):
                kind = jnp.where(role == 2, 3 * k, jnp.where(role == 1, 2, 5))
                b = jnp.where(role == 2, k, jnp.where(role == 1, 1, 0))
                send(box, slot(kind), source(b), way_y(kind))
        elif step == 1:
            @pl.when(role % 2 == 1)
            def _():
                kind = jnp.where(role == 1, 1, 4)
                send(box, slot(kind), source(role // 2), way_y(kind), add=slot(kind - 1))
        else:
            @pl.when(role == 0)
            def _():
                @pl.loop(0, 2)
                def _(b):
                    finish(box, source(b), slot(1 + 3 * b), slot(5 - 3 * b))

    def over_y_left(i, box, slot, r):
        role = (z + i - y + 4) % 4

        @pl.when(role == 2)
        def _():
            left_box(box, slot(0), r)
            left_box(box, slot(3), r)

        @pl.when(role % 2 == 1)
        def _():
            kind = jnp.where(role == 1, 1, 4)
            left_box(box, slot(kind), r)
            left_box(box, slot(kind + 1), r)

    def sends_left(phases):
        for i in range(4):
            for j in phases:
                over_y_left(i, box_y, lambda kind: 4 * kind + j, rows_y[i])

    def early_left():
        for swap in swaps:
            swap.wait_send()
        for j in range(4):
            for k in range(4):
                z_copy(j, k).wait_send()
                core_copy(j, k).wait_send()
        for i in range(4):
            @pl.loop(0, 6)
            def _(kind):
                left_box(box_x, kind * 4 + (z + i) % 4, rows_x[i])
        sends_left((0, 1, 2))

    def own_place(body):
        for i in range(4):
            @pl.when((y - z + 4) % 4 == i)
            def _(i=i):
                body(i)

    def own_rows(k):
        if ("rows", k) not in here:
            here.add(("rows", k))
            if k == 0:
                loads[0].wait()
                loads[1].wait()
            swaps[2 * k].wait_recv()
            swaps[2 * k + 1].wait_recv()

    def pieces_at(pieces):
        for j, i in pieces:
            core_copy(j, i).wait_recv()
        return pieces

    def last_x(k, i):
        if k == 0:
            @pl.loop(0, 2)
            def _(b):
                send(box_y, 24 + 3 * b, y_part(0, i, b), way_x(3 * b))
        elif k == 2:
            send(box_y, 26, y_part(1, i, 1), right)
        elif k == 5:
            send(box_y, 29, y_part(2, i, 0), left)
        elif k == 1:
            send(box_y, 25, y_part(1, i, 0), right, add=24)
        elif k == 4:
            send(box_y, 28, y_part(2, i, 1), left, add=27)
        else:
            @pl.loop(0, 2)
            def _(b):
                finish(box_y, y_part(3, i, b), 25 + 3 * b, 29 - 3 * b)

    def task(name, *index):
        k = index[0]
        if name == "left":
            early_left()
        elif name == "z":
            if k >= 2:
                near_here(k - 2)
            z_copy(k, 0).start()
            z_copy(k, 1).start()
        elif name == "pass":
            near_here(k)
            z_copy(k, 2).start()
            z_copy(k, 3).start()
        elif name == "near":
            near_here(k)
            core_copy(k, 3).start()
            core_copy(k, 1).start()
        elif name == "far":
            z_arrival(k, 2).wait_recv()
            z_arrival(k, 3).wait_recv()
            core_copy(k, 2).start()
        elif name == "own":
            pieces = [(2 * (k % 2), 0), (2 * (k % 2) + 1, 0)]
            own_rows(0)
            if k < 2:
                project(pieces_at(pieces), 0, 2 * rows_x[0])
            else:
                own_rows(1)
                project(pieces, 2 * rows_x[0], 2 * rows_y[0])
        elif name in ("pn", "pf"):
            own_rows(0)
            own_rows(1)
            project(pieces_at([(k, 3), (k, 1)] if name == "pn" else [(k, 2)]), 0, half)
        elif name == "xr":
            i = index[1]
            n = (z + i) % 4
            if k == 2:
                @pl.loop(0, 2)
                def _(b):
                    send(box_x, 12 * b + n, x_part(0, i, b), way_x(3 * b))
            elif k == 1:
                send(box_x, 8 + n, x_part(1, i, 1), right)
            else:
                send(box_x, 20 + n, x_part(2, i, 0), left)
        elif name == "xa":
            i = index[1]
            n = (z + i) % 4
            if k == 1:
                send(box_x, 4 + n, x_part(1, i, 0), right, add=n)
            else:
                send(box_x, 16 + n, x_part(2, i, 1), left, add=12 + n)
        elif name == "xf":
            n = (z + k) % 4

            @pl.loop(0, 2)
            def _(b):
                finish(box_x, x_part(3, k, b), 4 + 12 * b + n, 20 - 12 * b + n)
        elif name == "y":
            j, i = index[1:]
            over_y(k, i, box_y, lambda kind: 4 * kind + j, lambda b: y_part(j, i, b))
        elif name == "ly":
            i, c = index[1:]
            over_y(k, i, box_x, lambda kind: 24 + 6 * c + kind, lambda b: x_part(3, i, b, c, CUTS))
        else:
            own_place(functools.partial(last_x, k))

    right, left = at(dx=1), at(dx=-1)
    for name, *index in TASKS:
        task(name, *index)

    query = lax.broadcasted_iota(jnp.int32, (8, 128), 0)
    owner = lax.broadcasted_iota(jnp.int32, (8, 128), 1) // R

    mask = jnp.concatenate([
        jnp.where((owner == query + 2 * which) & (query < 2), 1.0, 0.0).astype(BF16) for which in (core, 1 - core)], axis=0)
    rows = half // 4
    for g in range(4):
        line = pl.ds(g * rows, rows)
        product = part[3, y, 0, line, :] * part[3, y, 1, line, :] * (1.0 / math.sqrt(R))
        high = product.astype(BF16)
        rest = product - high.astype(F32)
        middle = rest.astype(BF16)
        low = (rest - middle.astype(F32)).astype(BF16)
        total = None
        for term in (low, middle, high):
            s = lax.dot_general(mask, term, (((1,), (1,)), ((), ())), preferred_element_type=F32)
            total = s if total is None else total + s
        mine[0, :, line] = total[:8]
        theirs[0, :, line] = total[8:]
    final = copy(theirs.at[0], theirs.at[1], end_send, end_recv, at(other=True))
    final.start()
    out[:, pl.ds(pl.multiple_of(own, half), half)] = mine[0, pl.ds(0, 2), :]
    final.wait_recv()
    out[:, pl.ds(pl.multiple_of(partner_rows, half), half)] = theirs[1, pl.ds(0, 2), :]

    final.wait_send()
    sends_left((3,))
    for i in range(4):
        for c in range(CUTS):
            over_y_left(i, box_x, lambda kind: 24 + 6 * c + kind, rows_x[i] // CUTS)

    def last_left(i):
        @pl.loop(0, 6)
        def _(kind):
            left_box(box_y, 24 + kind, rows_y[i])

    own_place(last_left)


def scores_of(act, grad, q_in, q_out):
    tokens, w_in = act.shape
    w_out = grad.shape[1]
    half, wide = tokens // 2, w_in + w_out
    rx, ry = max(ROWS_X), half // 2 - min(ROWS_X)
    slots = 24 + 6 * CUTS
    dma = pltpu.SemaphoreType.DMA
    scores = pl.pallas_call(
        kernel,
        out_shape=jax.ShapeDtypeStruct((2, tokens), F32),
        in_specs=[pl.BlockSpec(memory_space=pl.ANY)] * 4,
        out_specs=pl.BlockSpec(memory_space=pltpu.VMEM),
        scratch_shapes=[
            pltpu.VMEM((half, 2 * wide), BF16),
            pltpu.VMEM((4, 4, 2 * wide, 128), BF16),
            pltpu.VMEM((4, 4, 2, half, 128), F32),
            pltpu.VMEM((slots, 2 * rx + 16, 128), BF16),
            pltpu.VMEM((slots, 2 * rx + 16, 128), BF16),
            pltpu.VMEM((30, 2 * ry + 16, 128), BF16),
            pltpu.VMEM((30, 2 * ry + 16, 128), BF16),
            pltpu.VMEM((2, 8, 128), F32),
            pltpu.VMEM((1, 8, half), F32),
            pltpu.VMEM((2, 8, half), F32),
            dma((10,)), dma((4,)), dma((4,)),
            dma((4, 4)), dma((4, 4)), dma((4, 4)), dma((4, 4)),
            dma((slots,)), dma((slots,)), dma((30,)), dma((30,)), dma, dma,
        ],
        compiler_params=pltpu.CompilerParams(
            collective_id=0, has_side_effects=True, vmem_limit_bytes=58 * 1024 * 1024),
        cost_estimate=pl.CostEstimate(flops=2 * tokens * wide * 2048, bytes_accessed=6 * 2**20, transcendentals=0),
    )(act, grad, q_in, q_out)
    return scores.T


def solution(mesh):
    return jax.shard_map(
        scores_of,
        mesh=mesh,
        in_specs=(P("dp", "tensor"), P("dp", "tensor"), P("tensor", "dp"), P("tensor", "dp")),
        out_specs=P("dp", "tensor"),
        check_vma=False,
    )
```

```python
import functools
import math

import jax
import jax.numpy as jnp
from jax import lax
from jax.experimental import pallas as pl
from jax.experimental.pallas import tpu as pltpu
from jax.sharding import PartitionSpec as P

R = 32
MESH = pl.DeviceIdType.MESH
BF16, F32 = jnp.bfloat16, jnp.float32
SPAN, LOW = 250.0, -124.0
ORDER = (2, 1, 3, 0)
ROWS_X = (320, 224, 384, 224)
CUTS = 1
TASKS = (
    ('own', 0), ('z', 1), ('xr', 2, 0), ('own', 1), ('own', 2), ('near', 0), ('xr', 1, 0), ('y', 0, 0, 0),
    ('xr', 3, 0), ('pn', 0), ('pass', 0), ('z', 2), ('xr', 2, 1), ('xa', 3, 0), ('y', 0, 0, 1), ('xa', 1, 0),
    ('y', 0, 0, 3), ('near', 1), ('y', 0, 1, 0), ('xr', 2, 3), ('pn', 1), ('y', 0, 1, 3), ('y', 0, 1, 1), ('own', 3),
    ('pass', 1), ('far', 0), ('y', 1, 0, 1), ('y', 1, 0, 3), ('y', 1, 0, 0), ('y', 0, 2, 0), ('pf', 0), ('xr', 2, 2),
    ('y', 0, 0, 2), ('near', 2), ('pass', 2), ('y', 0, 3, 0), ('z', 3), ('y', 1, 1, 1), ('xr', 1, 3), ('y', 1, 1, 3),
    ('xa', 1, 3), ('pn', 2), ('far', 1), ('xr', 3, 3), ('y', 0, 2, 1), ('y', 0, 2, 3), ('xf', 0), ('pf', 1),
    ('far', 2), ('xa', 3, 3), ('xr', 1, 2), ('y', 1, 2, 0), ('y', 1, 0, 2), ('y', 0, 1, 2), ('pf', 2), ('xr', 3, 2),
    ('y', 1, 3, 0), ('y', 2, 0, 1), ('y', 2, 0, 3), ('y', 0, 2, 2), ('xa', 3, 2), ('y', 2, 0, 0), ('pass', 3),
    ('near', 3), ('xa', 1, 2), ('y', 1, 1, 2), ('xa', 3, 1), ('y', 1, 2, 1), ('y', 1, 2, 3), ('xr', 3, 1),
    ('y', 1, 1, 0), ('y', 1, 2, 2), ('pn', 3), ('y', 0, 3, 1), ('y', 2, 2, 0), ('y', 0, 3, 3), ('xr', 1, 1),
    ('y', 2, 0, 2), ('y', 2, 1, 2), ('far', 3), ('xf', 3), ('y', 2, 2, 2), ('xa', 1, 1), ('pf', 3), ('y', 0, 3, 2),
    ('xf', 2), ('ly', 0, 2, 0), ('y', 2, 2, 1), ('ly', 0, 0, 0), ('y', 2, 2, 3), ('ly', 0, 3, 0), ('y', 2, 1, 3),
    ('y', 2, 3, 0), ('y', 2, 1, 0), ('lx', 0), ('xf', 1), ('ly', 0, 1, 0), ('y', 2, 1, 1), ('lx', 5), ('y', 1, 3, 1),
    ('lx', 2), ('ly', 1, 2, 0), ('y', 1, 3, 3), ('ly', 1, 0, 0), ('y', 1, 3, 2), ('lx', 4), ('ly', 1, 3, 0),
    ('lx', 1), ('ly', 1, 1, 0), ('left', 0), ('ly', 2, 2, 0), ('y', 2, 3, 1), ('ly', 2, 0, 0), ('y', 2, 3, 3),
    ('y', 2, 3, 2), ('lx', 9), ('ly', 2, 3, 0), ('ly', 2, 1, 0),
)


def encode(value, box, top_box):
    rows = value.shape[0]
    size = jnp.abs(value).reshape(rows // 8, 8, 128)
    top = jnp.max(size, axis=0).astype(BF16).astype(F32)
    top_box[...] = top
    part = size * (SPAN * SPAN / jnp.maximum(top, 1e-30))[None]
    root = part * lax.rsqrt(part + 1e-30)
    code = jnp.exp2(root + LOW).reshape(rows, 128)
    box[...] = jnp.where(value < 0, -code, code).astype(BF16)


def decode(box, top):
    rows = box.shape[0]
    code = box[...].astype(F32)
    root = jnp.log(jnp.abs(code)) * (1.0 / (SPAN * math.log(2.0))) - LOW / SPAN
    size = ((root * root).reshape(rows // 8, 8, 128) * top[None]).reshape(rows, 128)
    return jnp.where(code < 0, -size, size)


def kernel(
    act, grad, q_in, q_out, out,
    a, q, part, sent_x, got_x, sent_y, got_y, tops, mine, theirs,
    load_sem, a_send, a_recv, z_send, z_recv, core_send, core_recv,
    send_x_sem, recv_x_sem, send_y_sem, recv_y_sem, end_send, end_recv,
):
    box_x, box_y = (sent_x, got_x, send_x_sem, recv_x_sem), (sent_y, got_y, send_y_sem, recv_y_sem)
    z, t = lax.axis_index("dp"), lax.axis_index("tensor")
    core, x, y = t % 2, (t // 2) % 4, t // 8
    tokens, w_in = act.shape
    w_out = grad.shape[1]
    half, wide = tokens // 2, w_in + w_out
    rows_x = ROWS_X
    rows_y = tuple(half // 2 - r for r in ROWS_X)

    def at(dx=0, dy=0, dz=0, other=False):
        index = (((y + dy + 4) % 4) * 4 + (x + dx + 4) % 4) * 2 + ((1 - core) if other else core)
        return ((z + dz + 4) % 4, index)

    own, partner_rows = core * half, (1 - core) * half

    barrier = pltpu.get_barrier_semaphore()
    for device in (at(dx=1), at(dx=-1), at(dy=1), at(dy=-1), at(dz=1), at(dz=-1), at(other=True)):
        pl.semaphore_signal(barrier, inc=1, device_id=device, device_id_type=MESH)

    loads = [
        pltpu.make_async_copy(act.at[pl.ds(own, half), :], a.at[:, pl.ds(0, w_in)], load_sem.at[0]),
        pltpu.make_async_copy(grad.at[pl.ds(own, half), :], a.at[:, pl.ds(w_in, w_out)], load_sem.at[1]),
    ]
    for j, step in enumerate(ORDER):
        columns = pl.ds(pl.multiple_of(((x + step) % 4) * 128, 128), 128)
        loads.append(pltpu.make_async_copy(q_in.at[:, columns], q.at[j, z, pl.ds(0, w_in), :], load_sem.at[2 + 2 * j]))
        loads.append(pltpu.make_async_copy(q_out.at[:, columns], q.at[j, z, pl.ds(w_in, w_out), :], load_sem.at[3 + 2 * j]))
    for load in loads[2:] + loads[:2]:
        load.start()

    pl.semaphore_wait(barrier, 7)

    def copy(src, dst, send, recv, device):
        return pltpu.make_async_remote_copy(
            src_ref=src, dst_ref=dst, send_sem=send, recv_sem=recv, device_id=device, device_id_type=MESH)

    swaps = []
    for k, (low, count) in enumerate(((0, 2 * rows_x[0]), (2 * rows_x[0], 2 * rows_y[0]))):
        theirs_now = pl.ds(pl.multiple_of(partner_rows + low, 32), count)
        for h, (source, base, width) in enumerate(((act, wide, w_in), (grad, wide + w_in, w_out))):
            swaps.append(copy(source.at[theirs_now, :], a.at[pl.ds(low, count), pl.ds(base, width)],
                              a_send.at[2 * k + h], a_recv.at[2 * k + h], at(other=True)))

    def z_copy(j, kind):
        piece, low, count, dz = {
            0: (z, 0, wide, 1),
            1: (z, 0, wide, -1),
            2: ((z + 3) % 4, 0, wide // 2, 1),
            3: ((z + 1) % 4, wide // 2, wide // 2, -1),
        }[kind]
        ref = q.at[j, piece, pl.ds(low, count), :]
        return copy(ref, ref, z_send.at[j, kind], z_recv.at[j, kind], at(dz=dz))

    def z_arrival(j, kind):
        piece, low, count, dz = {
            0: ((z + 3) % 4, 0, wide, 1),
            1: ((z + 1) % 4, 0, wide, -1),
            2: ((z + 2) % 4, 0, wide // 2, 1),
            3: ((z + 2) % 4, wide // 2, wide // 2, -1),
        }[kind]
        ref = q.at[j, piece, pl.ds(low, count), :]
        return copy(ref, ref, z_send.at[j, kind], z_recv.at[j, kind], at(dz=dz))

    def core_copy(j, step):
        piece = (z + step) % 4
        return copy(q.at[j, piece, pl.ds(0, wide), :], q.at[j, piece, pl.ds(wide, wide), :],
                    core_send.at[j, step], core_recv.at[j, step], at(other=True))

    for j in range(4):
        loads[2 + 2 * j].wait()
        loads[3 + 2 * j].wait()
        if j == 0:
            z_copy(j, 0).start()
            z_copy(j, 1).start()
        core_copy(j, 0).start()
        if j == 0:
            swaps[0].start()
            swaps[1].start()
    swaps[2].start()
    swaps[3].start()

    here = set()

    def near_here(j):
        if j not in here:
            here.add(j)
            z_arrival(j, 0).wait_recv()
            z_arrival(j, 1).wait_recv()

    def project(pieces, first, count_of):
        block = count_of // 2

        @pl.loop(0, 2)
        def _(i):
            line = pl.ds(pl.multiple_of(first + i * block, 32), block)
            for h, (low, count) in enumerate(((0, w_in), (w_in, w_out))):
                bases = (low, low + wide)
                rows_of = jnp.concatenate([a[line, pl.ds(base, count)] for base in bases], axis=1)
                columns = [
                    jnp.concatenate([q[j, (z + step) % 4, pl.ds(base, count), :] for base in bases], axis=0) for j, step in pieces]
                columns = columns[0] if len(columns) == 1 else jnp.concatenate(columns, axis=1)
                total = jnp.dot(rows_of, columns, preferred_element_type=F32)
                for k, (j, step) in enumerate(pieces):
                    part[j, (z + step) % 4, h, line, :] = total[:, k * 128:(k + 1) * 128]

    def message(box, m, device, r):
        sent, got, out_sem, in_sem = box
        line = pl.ds(0, 2 * r + 16)
        return copy(sent.at[m, line, :], got.at[m, line, :], out_sem.at[m], in_sem.at[m], device)

    def arrived(box, m, r):
        message(box, m, at(dx=1), r).wait_recv()

    def left_box(box, m, r):
        message(box, m, at(dx=1), r).wait_send()

    def read(box, m, h, r):
        got = box[1]
        top = got[m, pl.ds(2 * r, 16), :].astype(F32).reshape(2, 8, 128)
        return decode(got.at[m, pl.ds(pl.multiple_of(h * r, 16), r), :], jnp.where(h == 0, top[0], top[1]))

    def send(box, m, source, device, add=None):
        sent, r = box[0], source.shape[1]
        if add is not None:
            arrived(box, add, r)

        @pl.loop(0, 2)
        def _(h):
            value = source[h]
            if add is not None:
                value = value + read(box, add, h, r)
            encode(value, sent.at[m, pl.ds(pl.multiple_of(h * r, 16), r), :], tops.at[h])

        sent[m, pl.ds(2 * r, 16), :] = tops[...].reshape(16, 128).astype(BF16)
        message(box, m, device, r).start()

    def finish(box, target, first, second):
        r = target.shape[1]
        arrived(box, first, r)
        arrived(box, second, r)

        @pl.loop(0, 2)
        def _(h):
            target[h] = target[h] + read(box, first, h, r) + read(box, second, h, r)

    def x_part(j, i, b, c=0, cuts=1):
        r = rows_x[i]
        return part.at[j, (z + i) % 4, :, pl.ds(pl.multiple_of(b * r + c * (r // cuts), 16), r // cuts), :]

    def y_part(j, i, b):
        r = rows_y[i]
        return part.at[j, (z + i) % 4, :, pl.ds(pl.multiple_of(2 * rows_x[i] + b * r, 16), r), :]

    def way_x(kind):
        return at(dx=jnp.where(kind < 3, 1, -1))

    def way_y(kind):
        return at(dy=jnp.where(kind < 3, 1, -1))

    def over_y(step, i, box, slot, source):
        role = (z + i - y + 4) % 4
        if step == 0:
            @pl.loop(0, jnp.where(role == 2, 2, jnp.where(role == 0, 0, 1)))
            def _(k):
                kind = jnp.where(role == 2, 3 * k, jnp.where(role == 1, 2, 5))
                b = jnp.where(role == 2, k, jnp.where(role == 1, 1, 0))
                send(box, slot(kind), source(b), way_y(kind))
        elif step == 1:
            @pl.when(role % 2 == 1)
            def _():
                kind = jnp.where(role == 1, 1, 4)
                send(box, slot(kind), source(role // 2), way_y(kind), add=slot(kind - 1))
        else:
            @pl.when(role == 0)
            def _():
                @pl.loop(0, 2)
                def _(b):
                    finish(box, source(b), slot(1 + 3 * b), slot(5 - 3 * b))

    def over_y_left(i, box, slot, r):
        role = (z + i - y + 4) % 4

        @pl.when(role == 2)
        def _():
            left_box(box, slot(0), r)
            left_box(box, slot(3), r)

        @pl.when(role % 2 == 1)
        def _():
            kind = jnp.where(role == 1, 1, 4)
            left_box(box, slot(kind), r)
            left_box(box, slot(kind + 1), r)

    def sends_left(phases):
        for i in range(4):
            for j in phases:
                over_y_left(i, box_y, lambda kind: 4 * kind + j, rows_y[i])

    def early_left():
        for swap in swaps:
            swap.wait_send()
        for j in range(4):
            for k in range(4):
                z_copy(j, k).wait_send()
                core_copy(j, k).wait_send()
        for i in range(4):
            @pl.loop(0, 6)
            def _(kind):
                left_box(box_x, kind * 4 + (z + i) % 4, rows_x[i])
        sends_left((0, 1, 2))

    def own_place(body):
        for i in range(4):
            @pl.when((y - z + 4) % 4 == i)
            def _(i=i):
                body(i)

    def own_rows(k):
        if ("rows", k) not in here:
            here.add(("rows", k))
            if k == 0:
                loads[0].wait()
                loads[1].wait()
            swaps[2 * k].wait_recv()
            swaps[2 * k + 1].wait_recv()

    def pieces_at(pieces):
        for j, i in pieces:
            core_copy(j, i).wait_recv()
        return pieces

    def last_x(k, i):
        if k == 0:
            @pl.loop(0, 2)
            def _(b):
                send(box_y, 24 + 3 * b, y_part(0, i, b), way_x(3 * b))
        elif k == 2:
            send(box_y, 26, y_part(1, i, 1), right)
        elif k == 5:
            send(box_y, 29, y_part(2, i, 0), left)
        elif k == 1:
            send(box_y, 25, y_part(1, i, 0), right, add=24)
        elif k == 4:
            send(box_y, 28, y_part(2, i, 1), left, add=27)
        else:
            @pl.loop(0, 2)
            def _(b):
                finish(box_y, y_part(3, i, b), 25 + 3 * b, 29 - 3 * b)

    query = lax.broadcasted_iota(jnp.int32, (8, 128), 0)
    owner = lax.broadcasted_iota(jnp.int32, (8, 128), 1) // R

    mask = jnp.concatenate([
        jnp.where((owner == query + 2 * which) & (query < 2), 1.0, 0.0).astype(BF16) for which in (core, 1 - core)], axis=0)
    rows = half // 4

    def score(g):
        line = pl.ds(g * rows, rows)
        product = part[3, y, 0, line, :] * part[3, y, 1, line, :] * (1.0 / math.sqrt(R))
        high = product.astype(BF16)
        rest = product - high.astype(F32)
        middle = rest.astype(BF16)
        low = (rest - middle.astype(F32)).astype(BF16)
        total = None
        for term in (low, middle, high):
            s = lax.dot_general(mask, term, (((1,), (1,)), ((), ())), preferred_element_type=F32)
            total = s if total is None else total + s
        mine[0, :, line] = total[:8]
        theirs[0, :, line] = total[8:]

    def task(name, *index):
        k = index[0]
        if name == "left":
            early_left()
        elif name == "z":
            if k >= 2:
                near_here(k - 2)
            z_copy(k, 0).start()
            z_copy(k, 1).start()
        elif name == "pass":
            near_here(k)
            z_copy(k, 2).start()
            z_copy(k, 3).start()
        elif name == "near":
            near_here(k)
            core_copy(k, 3).start()
            core_copy(k, 1).start()
        elif name == "far":
            z_arrival(k, 2).wait_recv()
            z_arrival(k, 3).wait_recv()
            core_copy(k, 2).start()
        elif name == "own":
            pieces = [(2 * (k % 2), 0), (2 * (k % 2) + 1, 0)]
            own_rows(0)
            if k < 2:
                project(pieces_at(pieces), 0, 2 * rows_x[0])
            else:
                own_rows(1)
                project(pieces, 2 * rows_x[0], 2 * rows_y[0])
        elif name in ("pn", "pf"):
            own_rows(0)
            own_rows(1)
            project(pieces_at([(k, 3), (k, 1)] if name == "pn" else [(k, 2)]), 0, half)
        elif name == "xr":
            i = index[1]
            n = (z + i) % 4
            if k == 2:
                @pl.loop(0, 2)
                def _(b):
                    send(box_x, 12 * b + n, x_part(0, i, b), way_x(3 * b))
            elif k == 1:
                send(box_x, 8 + n, x_part(1, i, 1), right)
            else:
                send(box_x, 20 + n, x_part(2, i, 0), left)
        elif name == "xa":
            i = index[1]
            n = (z + i) % 4
            if k == 1:
                send(box_x, 4 + n, x_part(1, i, 0), right, add=n)
            else:
                send(box_x, 16 + n, x_part(2, i, 1), left, add=12 + n)
        elif name == "xf":
            n = (z + k) % 4

            @pl.loop(0, 2)
            def _(b):
                finish(box_x, x_part(3, k, b), 4 + 12 * b + n, 20 - 12 * b + n)
        elif name == "y":
            j, i = index[1:]
            over_y(k, i, box_y, lambda kind: 4 * kind + j, lambda b: y_part(j, i, b))
        elif name == "ly":
            i, c = index[1:]
            over_y(k, i, box_x, lambda kind: 24 + 6 * c + kind, lambda b: x_part(3, i, b, c, CUTS))
        else:
            own_place(functools.partial(last_x, k))
            if k == 9:
                score(3)

    right, left = at(dx=1), at(dx=-1)
    for name, *index in TASKS:
        task(name, *index)
    for g in range(3):
        score(g)
    final = copy(theirs.at[0], theirs.at[1], end_send, end_recv, at(other=True))
    final.start()
    out[:, pl.ds(pl.multiple_of(own, half), half)] = mine[0, pl.ds(0, 2), :]
    sends_left((3,))
    for i in range(4):
        for c in range(CUTS):
            over_y_left(i, box_x, lambda kind: 24 + 6 * c + kind, rows_x[i] // CUTS)

    def last_left(i):
        @pl.loop(0, 6)
        def _(kind):
            left_box(box_y, 24 + kind, rows_y[i])

    own_place(last_left)
    final.wait_recv()
    out[:, pl.ds(pl.multiple_of(partner_rows, half), half)] = theirs[1, pl.ds(0, 2), :]
    final.wait_send()


def scores_of(act, grad, q_in, q_out):
    tokens, w_in = act.shape
    w_out = grad.shape[1]
    half, wide = tokens // 2, w_in + w_out
    rx, ry = max(ROWS_X), half // 2 - min(ROWS_X)
    slots = 24 + 6 * CUTS
    dma = pltpu.SemaphoreType.DMA
    scores = pl.pallas_call(
        kernel,
        out_shape=jax.ShapeDtypeStruct((2, tokens), F32),
        in_specs=[pl.BlockSpec(memory_space=pl.ANY)] * 4,
        out_specs=pl.BlockSpec(memory_space=pltpu.VMEM),
        scratch_shapes=[
            pltpu.VMEM((half, 2 * wide), BF16),
            pltpu.VMEM((4, 4, 2 * wide, 128), BF16),
            pltpu.VMEM((4, 4, 2, half, 128), F32),
            pltpu.VMEM((slots, 2 * rx + 16, 128), BF16),
            pltpu.VMEM((slots, 2 * rx + 16, 128), BF16),
            pltpu.VMEM((30, 2 * ry + 16, 128), BF16),
            pltpu.VMEM((30, 2 * ry + 16, 128), BF16),
            pltpu.VMEM((2, 8, 128), F32),
            pltpu.VMEM((1, 8, half), F32),
            pltpu.VMEM((2, 8, half), F32),
            dma((10,)), dma((4,)), dma((4,)),
            dma((4, 4)), dma((4, 4)), dma((4, 4)), dma((4, 4)),
            dma((slots,)), dma((slots,)), dma((30,)), dma((30,)), dma, dma,
        ],
        compiler_params=pltpu.CompilerParams(
            collective_id=0, has_side_effects=True, vmem_limit_bytes=58 * 1024 * 1024),
        cost_estimate=pl.CostEstimate(flops=2 * tokens * wide * 2048, bytes_accessed=6 * 2**20, transcendentals=0),
    )(act, grad, q_in, q_out)
    return scores.T


def solution(mesh):
    return jax.shard_map(
        scores_of,
        mesh=mesh,
        in_specs=(P("dp", "tensor"), P("dp", "tensor"), P("tensor", "dp"), P("tensor", "dp")),
        out_specs=P("dp", "tensor"),
        check_vma=False,
    )
```
